256 devices in a mesh: item: 128 (over y, z_hi, x, core), batch: 2 (over z_lo).
Axes of the slice: x: 4, y: 4, z: 8 (z_hi: 4, z_lo: 2; z = z_hi * 2 + z_lo), core: 2. Of those that a mesh axis runs over, the one named last changes fastest.
Arguments:
- user_vectors: bfloat16 [32768, 256], P(('item', 'batch')), may hold values from -70 to 70
- item_table: float32 [262144, 256], P('item'), may hold values from -0.3 to 0.3
- grad_accum: float32 [262144, 256], P('item'), may hold values from 0.05 to 0.5
- log_prob: float32 [262144], P('item'), may hold values from -16 to -6
- positive_shard: int32 [32768, 1], P(('item', 'batch')), may hold values from 0 to 127; in each aligned block of 128 rows (0 to 127, 128 to 255, ...) at most 2 rows name the same one
- positive_row: int32 [32768], P(('item', 'batch')), may hold values from 0 to 2047
- negatives: int32 [65536], P('item'), may hold values from 0 to 2047
Outputs:
- new_table: float32 [262144, 256], P('item')
- new_accum: float32 [262144, 256], P('item')
- user_loss: float32 [32768], P(('item', 'batch'))
The draws below stay inside these ranges and needn't reach their ends.
Inputs may be any that keep to these rules, and one draw needn't show every extreme that they name: `positive_shard`: in the 128 user rows of one device at most 2 name one shard, and exactly 2 do for some shard.
All inputs are finite; a program needn't handle non-finite values.
Results may differ from the reference program's by a relative error of at most 0.0046.
Values may be sent and summed in bfloat16 or wider, within the bound.
A program may use at most 192 MiB of HBM per device.

```python
import math
import jax
import jax.numpy as jnp
import numpy as np
from jax import lax

D = 256
ITEM_DEV = 2048
USER_DEV = 128
NEG_DEV = 512
CAP = 2
USERS = 32768
ITEMS = 262144
NEGS = 65536
N_ITEM = 128


def draw_user_vectors(key, part):
    key = jax.random.fold_in(key, 11)
    key_values = jax.random.fold_in(key, 0)
    values = jnp.clip(jax.random.normal(key_values, (USERS, D), jnp.float32), -4.0, 4.0)
    return values.astype(jnp.bfloat16)


def place_ends(array, own_key, low, high):
    dims = array.shape
    place = [jax.random.randint(jax.random.fold_in(own_key, axis), (), 0, dims[axis]) for axis in range(len(dims))]
    array = array.at[tuple(place)].set(low)
    longest = dims.index(max(dims))
    place[longest] = (place[longest] + 1) % dims[longest]
    return array.at[tuple(place)].set(high)


def level_of(own_key, shape, cuts, least, high):
    level, own = 1.0, jax.random.fold_in(own_key, 6)
    for dim, shards_of in cuts:
        draws = jnp.exp(jax.random.uniform(jax.random.fold_in(own, dim), (shards_of,), jnp.float32, least / len(cuts), high / len(cuts)))
        level = level * jnp.repeat(draws, shape[dim] // shards_of).reshape([-1 if axis == dim else 1 for axis in range(len(shape))])
    return level


def shared_out(own_key, own, number, rows, amount, top, bound, slope):
    ranking = jax.random.permutation(own_key, amount)
    packed, usual = portions_of(amount, rows * top, bound, slope, True), portions_of(amount, rows * top, bound, slope, False)
    places = jnp.arange(amount)

    def named(tallies, turn):
        used = int((tallies > 0).sum())
        fixed = max(1, used // 4)
        shifted = fixed + (places - fixed + turn * (used - fixed)) % max(1, amount - fixed)
        return jnp.zeros((amount,), jnp.int32).at[ranking[jnp.where(places < fixed, places, shifted)]].set(jnp.asarray(tallies, jnp.int32))

    tallies = jnp.where(number % 4 == 0, named(packed, number // 4), named(usual, number - number // 4 - 1))
    mixed = jax.random.permutation(jax.random.fold_in(own, 3), amount)
    source_of, sink = mixed[0:amount // 2 * 2:2], mixed[1:amount // 2 * 2:2]
    room = jnp.minimum(tallies[source_of] - 1, bound - tallies[sink]) // 2
    room = jnp.where((source_of == ranking[0]) | (sink == ranking[0]) | (tallies[sink] == 0), 0, jnp.maximum(room, 0))
    shifted = jax.random.randint(jax.random.fold_in(own, 4), (amount // 2,), 0, 1 << 20) % (room + 1)
    tallies = tallies.at[source_of].add(-shifted).at[sink].add(shifted)
    items = jnp.searchsorted(jnp.cumsum(tallies), jnp.arange(rows * top), side="right").astype(jnp.int32)
    table = items.reshape(top, rows).T
    table = table[jax.random.permutation(jax.random.fold_in(own, 1), rows)]
    turn = jax.random.randint(jax.random.fold_in(own, 2), (rows, 1), 0, top)
    return jnp.take_along_axis(table, (jnp.arange(top)[None, :] + turn) % top, axis=1)


def portions_of(count, total, reach, skew, full):
    loads = [(1 << 20) // math.isqrt(standing ** skew) + 1 for standing in range(1, count + 1)]
    largest = reach if full else min(reach, max(-(-total // count), total * loads[0] // sum(loads)))
    least = 1 if total - largest >= count - 1 else 0
    holding, rest = [largest] + [least] * (count - 1), total - largest - least * (count - 1)
    while rest > 0:
        movable = [i for i in range(1, count) if holding[i] < largest] or [i for i in range(1, count) if holding[i] < reach]
        mass, left = sum([loads[i] for i in movable]), rest
        for i in movable:
            extra = min(reach - holding[i], max(1, left * loads[i] // mass), rest)
            holding[i] = holding[i] + extra
            rest = rest - extra
    return np.array(holding)


def bell_draw(stream_key, dims, spread, limit, cuts=(), held_as=jnp.bfloat16):
    factor_of = level_of(stream_key, dims, cuts, -0.22, 0.18) if cuts else 1.0
    entries = jax.random.normal(stream_key, dims, jnp.float32) * spread * factor_of
    return jnp.minimum(jnp.maximum(entries, -limit), limit).astype(held_as)


def setup_inputs(seed: int = 0) -> dict:
    keys = jax.random.split(jax.random.key(seed), 8)
    user_vectors = draw_user_vectors(jax.random.fold_in(keys[7], 71), 0)
    item_table = bell_draw(keys[1], (ITEMS, D), 0.05, 0.3, ((0, 128),), jnp.float32)
    grad_accum = jnp.clip(jnp.exp(math.log(0.5) - 2.3025851 * jax.random.uniform(keys[2], (ITEMS, D), jnp.float32) ** level_of(keys[2], (ITEMS, D), ((0, 128),), -0.2, 0.2)), 0.05, 0.5)
    log_prob = jnp.clip(-16.0 + 10.0 * jax.random.uniform(keys[3], (ITEMS,), jnp.float32) ** level_of(keys[3], (ITEMS,), ((0, 128),), -0.2, 0.2), -16.0, -6.0)
    positive_shard_keys = jax.random.split(jax.random.fold_in(keys[4], 1), USERS // USER_DEV)
    positive_shard_turns = jax.random.permutation(jax.random.fold_in(keys[4], 3), USERS // USER_DEV)
    positive_shard = jax.vmap(lambda own, number: shared_out(jax.random.fold_in(keys[4], 2), own, number, USER_DEV, N_ITEM, 1, CAP, 2))(positive_shard_keys, positive_shard_turns).reshape((USERS, 1))
    positive_row = place_ends(jax.random.randint(keys[5], (USERS,), 0, ITEM_DEV), jax.random.fold_in(keys[5], 1), 0, ITEM_DEV - 1).astype(jnp.int32)
    negatives = place_ends(jax.random.randint(keys[6], (NEGS,), 0, ITEM_DEV), jax.random.fold_in(keys[6], 1), 0, ITEM_DEV - 1).astype(jnp.int32)
    return {"user_vectors": user_vectors, "item_table": item_table, "grad_accum": grad_accum, "log_prob": log_prob, "positive_shard": positive_shard, "positive_row": positive_row, "negatives": negatives}


LOGIT_SCALE = 2.5
STEP_RATE = 0.05

def reference(user_vectors, item_table, grad_accum, log_prob, positive_shard, positive_row, negatives):
    shard_of = jnp.arange(NEGS, dtype=jnp.int32) // NEG_DEV
    neg_ids = (shard_of * ITEM_DEV + negatives).astype(jnp.int32)
    neg_rows = lax.optimization_barrier(item_table[neg_ids].astype(jnp.bfloat16)).astype(jnp.float32)
    neg_bias = log_prob[neg_ids]
    pos_ids = (positive_shard[:, 0] * ITEM_DEV + positive_row).astype(jnp.int32)
    users_wide = user_vectors.astype(jnp.float32)
    pos_vec = lax.optimization_barrier(item_table[pos_ids].astype(jnp.bfloat16)).astype(jnp.float32)
    pos_score = LOGIT_SCALE * lax.optimization_barrier(jnp.sum(users_wide * pos_vec, axis=1)) - log_prob[pos_ids]
    blocks = users_wide.reshape(USERS // USER_DEV, USER_DEV, D)

    def score_block(user_block):
        return LOGIT_SCALE * jnp.dot(user_block, neg_rows.T, preferred_element_type=jnp.float32) - neg_bias[None, :]

    def statistics(user_block):
        score_tile = score_block(user_block)
        tile_max = lax.optimization_barrier(jnp.max(score_tile, axis=1))
        tile_sum = lax.optimization_barrier(jnp.sum(jnp.exp(score_tile - tile_max[:, None]), axis=1))
        return (tile_max, tile_sum)
    tile_max, tile_sum = lax.map(statistics, blocks)
    tile_max = tile_max.reshape(USERS)
    tile_sum = tile_sum.reshape(USERS)
    peak_score = jnp.maximum(tile_max, pos_score)
    grand_total = tile_sum * jnp.exp(tile_max - peak_score) + jnp.exp(pos_score - peak_score)
    log_norm = peak_score + jnp.log(grand_total)
    user_loss = log_norm - pos_score
    coefficient = jnp.exp(pos_score - log_norm) - 1.0

    def grad_step(running, inputs):
        user_block, norm_block = inputs
        probs = jnp.exp(score_block(user_block) - norm_block[:, None])
        probs = lax.optimization_barrier(probs.astype(jnp.bfloat16)).astype(jnp.float32)
        return (running + jnp.dot(probs.T, user_block, preferred_element_type=jnp.float32), None)
    neg_sum, _ = lax.scan(grad_step, jnp.zeros((NEGS, D), jnp.float32), (blocks, log_norm.reshape(USERS // USER_DEV, USER_DEV)))
    grad = jnp.zeros_like(item_table).at[neg_ids].add(LOGIT_SCALE * neg_sum)
    grad = grad.at[pos_ids].add((LOGIT_SCALE * coefficient)[:, None] * users_wide)
    new_accum = grad_accum + grad * grad
    new_table = item_table - STEP_RATE * grad * lax.rsqrt(new_accum)
    return (new_table, new_accum, user_loss)
```

```python
import math

import jax
import jax.numpy as jnp
from jax import lax
from jax.experimental import pallas as pl
from jax.experimental.pallas import tpu as pltpu
from jax.sharding import PartitionSpec as P

LOGIT_SCALE = 2.5
STEP_RATE = 0.05
LOG2E = math.log2(math.e)
LN2 = math.log(2.0)
FLOOR = -1e30

BLOCKS = 128
ROWS = 128
WIDTH = 256
ITEMS = 2048
NEGS = 512
STEPS = 64
SLOTS = 256


def order4(q):
    return jnp.where(q < 2, q, 5 - q)


def head_kernel(
    u_ref, ids_ref, negr_ref, lp_ref, table_ref,
    gsum_ref, up_out, r_out, c_out, loss_ref,
    users, scores, negs, bias, tab, tabb, ids_all, first_i, last_i, first_r, last_r,
    slot_i, slot_r, slot_t, slot_lp, slot_pos, slot_u, slot_c,
    stat_out, stat_in, norm_all, acc, gsend, grecv, upx, rx, cx,
    block_sem, send_sem, tab_sem, ids_sem, ids_send, stat_sem, stat_send, norm_sem, norm_send,
    pair_send, pair_recv,
):
    me = lax.axis_index("item")
    group = lax.axis_index("batch")
    other = 1 - group
    core = lax.rem(me, 2)
    sib = me + 1 - 2 * core
    x_pos = lax.rem(me // 2, 4)
    z_pos = lax.rem(me // 8, 4)
    y_pos = me // 32
    outer = jnp.where(core == 0, y_pos, x_pos)
    inner = jnp.where(core == 0, x_pos, y_pos)
    s_out = jnp.where(core == 0, 32, 2)
    s_in = 34 - s_out

    def place(do, di, dz):
        return (
            lax.rem(outer + do, 4) * s_out + lax.rem(inner + di, 4) * s_in
            + lax.rem(z_pos + dz, 4) * 8 + core
        )

    def sib_place(do, di, dz):
        return (
            lax.rem(inner + do, 4) * s_in + lax.rem(outer + di, 4) * s_out
            + lax.rem(z_pos + dz, 4) * 8 + 1 - core
        )

    def parts(t):
        late = jnp.maximum(t - 16, 0)
        k = jnp.where(t < 16, t, jnp.where(t < 48, late // 2, t - 48))
        do = jnp.where(t < 16, 0, jnp.where(t < 48, 1 + 2 * lax.rem(late, 2), 2))
        return do, k // 4, lax.rem(k, 4), k

    def block_copy(b, dev):
        return pltpu.make_async_remote_copy(
            src_ref=users.at[b], dst_ref=users.at[b], send_sem=send_sem,
            recv_sem=block_sem.at[b], device_id={"item": dev},
            device_id_type=pl.DeviceIdType.MESH,
        )

    def forward(t):
        do, ki, kz, k = parts(t)
        di, dz = order4(ki), order4(kz)
        b = place(do, di, dz)

        @pl.when(t > 0)
        def _():
            block_copy(b, sib).wait_recv()

        @pl.when(do == 0)
        def _():
            block_copy(b, place(1, 0, 0)).start()
            block_copy(b, place(3, 0, 0)).start()

            @pl.when(di == 0)
            def _():
                block_copy(b, place(0, 1, 0)).start()
                block_copy(b, place(0, 3, 0)).start()

                @pl.when(dz == 0)
                def _():
                    block_copy(b, place(0, 0, 1)).start()
                    block_copy(b, place(0, 0, 3)).start()

                @pl.when(dz == 1 + 2 * core)
                def _():
                    block_copy(b, place(0, 0, 3 - 2 * core)).start()

            @pl.when((di == 1) & (lax.rem(kz, 2) == 0))
            def _():
                block_copy(b, place(0, 3, 0)).start()

            @pl.when((di == 3) & (lax.rem(kz, 2) == 1))
            def _():
                block_copy(b, place(0, 1, 0)).start()

        @pl.when((do == 1) & (lax.rem(k, 2) == 0))
        def _():
            block_copy(b, place(3, 0, 0)).start()

        @pl.when((do == 3) & (lax.rem(k, 2) == 1))
        def _():
            block_copy(b, place(1, 0, 0)).start()

        block_copy(b, sib).start()

    def blocks_of(t):
        do, ki, kz, _ = parts(t)
        di, dz = order4(ki), order4(kz)
        return place(do, di, dz), sib_place(do, di, dz)

    def peer_copy(src, dst, send, recv, dev):
        return pltpu.make_async_remote_copy(
            src_ref=src, dst_ref=dst, send_sem=send, recv_sem=recv,
            device_id={"item": dev}, device_id_type=pl.DeviceIdType.MESH,
        )

    def wait_bytes(ref, sem):
        pltpu.make_async_copy(ref, ref, sem).wait()

    table_copy = pltpu.make_async_copy(table_ref, tab, tab_sem)
    table_copy.start()
    users[me] = u_ref[...]
    ids_all[me] = ids_ref[...]
    forward(jnp.int32(0))

    @pl.loop(1, BLOCKS)
    def _(j):
        dev = lax.rem(me + j, BLOCKS)
        peer_copy(ids_all.at[me], ids_all.at[me], ids_send, ids_sem, dev).start()

    @pl.loop(1, 4)
    def _(t):
        forward(t)

    table_copy.wait()
    tabb[...] = tab[...].astype(jnp.bfloat16)
    lp2 = lp_ref[...] * LOG2E

    def hot_of(row_cols):
        lane = lax.broadcasted_iota(jnp.int32, row_cols.shape, 1)
        return [row_cols == lane + 128 * j for j in range(ITEMS // 128)]

    def gather(row_cols):
        hots = hot_of(row_cols)
        hot = jnp.concatenate([h.astype(jnp.float32).astype(jnp.bfloat16) for h in hots], axis=1)
        rows = jnp.dot(hot, tabb[...], preferred_element_type=jnp.float32)
        total = jnp.zeros(row_cols.shape, jnp.float32)
        for j, h in enumerate(hots):
            total = total + jnp.where(h, lp2[:, 128 * j : 128 * (j + 1)], 0.0)
        lp_rows = jnp.broadcast_to(jnp.sum(total, axis=1, keepdims=True), row_cols.shape)
        return rows, lp_rows

    neg_cols = jnp.transpose(jnp.broadcast_to(negr_ref[...], (128, NEGS)))
    for q in range(NEGS // 128):
        part = slice(128 * q, 128 * (q + 1))
        rows, lp_rows = gather(neg_cols[part])
        negs[part, :] = rows.astype(jnp.bfloat16)
        bias[part, :] = lp_rows

    @pl.loop(4, 16)
    def _(t):
        forward(t)

    wait_bytes(ids_all.at[pl.ds(0, BLOCKS - 1)], ids_sem)
    ids = ids_all[:, 0, :]
    lane = lax.broadcasted_iota(jnp.int32, (BLOCKS, ROWS), 1)
    mine = (ids // ITEMS) == me
    row = lax.rem(ids, ITEMS)
    wide = (BLOCKS, ROWS)
    lo = jnp.broadcast_to(
        jnp.min(jnp.where(mine, lane, ROWS), axis=1, keepdims=True), wide
    )
    hi = jnp.broadcast_to(jnp.max(jnp.where(mine, lane, -1), axis=1, keepdims=True), wide)
    first_i[...] = jnp.where(lo < ROWS, lo, -1)
    last_i[...] = jnp.where(hi > lo, hi, -1)
    first_r[...] = jnp.broadcast_to(
        jnp.max(jnp.where(mine & (lane == lo), row, -1), axis=1, keepdims=True), wide
    )
    last_r[...] = jnp.broadcast_to(
        jnp.max(jnp.where(mine & (lane == hi) & (hi > lo), row, -1), axis=1, keepdims=True), wide
    )
    sub = lax.broadcasted_iota(jnp.int32, (8, 128), 0)

    @pl.loop(0, STEPS // 2)
    def _(i):
        ivals, rvals = [], []
        for u in range(2):
            for b in blocks_of(2 * i + u):
                ivals += [first_i[pl.ds(b, 1), :], last_i[pl.ds(b, 1), :]]
                rvals += [first_r[pl.ds(b, 1), :], last_r[pl.ds(b, 1), :]]
        islab = jnp.broadcast_to(ivals[0], (8, 128))
        rslab = jnp.broadcast_to(rvals[0], (8, 128))
        for c in range(1, 8):
            islab = jnp.where(sub == c, ivals[c], islab)
            rslab = jnp.where(sub == c, rvals[c], rslab)
        slot_i[pl.ds(8 * i, 8), :] = islab
        slot_r[pl.ds(8 * i, 8), :] = rslab

    for q in range(SLOTS // 128):
        part = slice(128 * q, 128 * (q + 1))
        rows, lp_rows = gather(slot_r[part, :])
        slot_t[part, :] = rows
        slot_lp[part, :] = lp_rows

    lane8 = lax.broadcasted_iota(jnp.int32, (8, 128), 1)

    def slot_masks(i, u):
        islab = slot_i[pl.ds(8 * i, 8), :]
        hit = islab == lane8
        left = hit & (sub >= 4 * u) & (sub < 4 * u + 2)
        right = hit & (sub >= 4 * u + 2) & (sub < 4 * u + 4)
        return jnp.concatenate(
            [jnp.where(left, 1.0, 0.0), jnp.where(right, 1.0, 0.0)], axis=1
        )

    def two_blocks(t):
        b1, b2 = blocks_of(t)
        return jnp.concatenate([users[b1], users[b2]], axis=0)

    def send_stats(b, lse, pos):
        stat_out[b] = jnp.concatenate([lse, pos], axis=0)

        @pl.when(b != me)
        def _():
            peer_copy(stat_out.at[b], stat_in.at[me], stat_send, stat_sem, b).start()

        @pl.when(b == me)
        def _():
            stat_in[b] = stat_out[b]

    @pl.loop(0, STEPS // 2)
    def _(i):
        phase = lax.rem(i, 4)

        @pl.when(phase < 3)
        def _():
            pair = 8 + 3 * (i // 4) + phase
            forward(2 * pair)
            forward(2 * pair + 1)

        gathered = jnp.zeros((8, WIDTH), jnp.float32)
        masks = []
        for u in range(2):
            t = 2 * i + u
            b1, b2 = blocks_of(t)
            block_copy(b2, sib).wait_recv()
            pair_users = jnp.concatenate([users[b1], users[b2]], axis=0)
            mask = slot_masks(i, u)
            masks.append(mask)
            hot = jnp.concatenate([mask, jnp.zeros_like(mask)], axis=0).astype(jnp.bfloat16)
            gathered = gathered + jnp.dot(
                hot, pair_users, preferred_element_type=jnp.float32
            )[0:8]
            raw = lax.dot_general(
                negs[...], pair_users, (((1,), (1,)), ((), ())),
                preferred_element_type=jnp.float32,
            )
            cols = jnp.concatenate([bias[...], bias[...]], axis=1)
            scaled = raw * (LOGIT_SCALE * LOG2E) - cols
            scores[t] = scaled
        slot_u[pl.ds(8 * i, 8), :] = gathered
        dots = jnp.sum(gathered * slot_t[pl.ds(8 * i, 8), :], axis=1, keepdims=True)
        pos = dots * (LOGIT_SCALE * LOG2E) - slot_lp[pl.ds(8 * i, 8), :]
        slot_pos[pl.ds(8 * i, 8), :] = pos
        pos_wide = jnp.concatenate([pos, pos], axis=1)
        for u in range(2):
            t = 2 * i + u
            b1, b2 = blocks_of(t)
            peak = jnp.max(scores[t], axis=0, keepdims=True)
            total = jnp.sum(jnp.exp2(scores[t] - peak), axis=0, keepdims=True)
            lse = peak + jnp.log(total) * LOG2E
            pos_row = jnp.max(
                jnp.where(masks[u] > 0.0, pos_wide, FLOOR), axis=0, keepdims=True
            )
            send_stats(b1, lse[:, :ROWS], pos_row[:, :ROWS])
            send_stats(b2, lse[:, ROWS:], pos_row[:, ROWS:])

    def pair_copy(src, dst, k):
        return pltpu.make_async_remote_copy(
            src_ref=src, dst_ref=dst, send_sem=pair_send.at[k], recv_sem=pair_recv.at[k],
            device_id={"batch": other}, device_id_type=pl.DeviceIdType.MESH,
        )

    upx[group] = slot_u[...].astype(jnp.bfloat16)
    rx[group] = jnp.transpose(slot_r[...])[0:8, :]
    up_copy = pair_copy(upx.at[group], upx.at[group], 0)
    r_copy = pair_copy(rx.at[group], rx.at[group], 1)
    up_copy.start()
    r_copy.start()

    wait_bytes(stat_in.at[pl.ds(0, BLOCKS - 1)], stat_sem)
    lses = stat_in[:, 0, :]
    pos_own = jnp.max(stat_in[:, 1, :], axis=0, keepdims=True)
    top = jnp.maximum(jnp.max(lses, axis=0, keepdims=True), pos_own)
    total = jnp.sum(jnp.exp2(lses - top), axis=0, keepdims=True) + jnp.exp2(pos_own - top)
    norm = top + jnp.log(total) * LOG2E
    norm_all[me] = norm

    @pl.loop(1, BLOCKS)
    def _(j):
        dev = lax.rem(me + j, BLOCKS)
        peer_copy(norm_all.at[me], norm_all.at[me], norm_send, norm_sem, dev).start()

    loss_ref[...] = (norm - pos_own) * LN2
    wait_bytes(norm_all.at[pl.ds(0, BLOCKS - 1)], norm_sem)

    def norm_row(t):
        b1, b2 = blocks_of(t)
        return jnp.concatenate([norm_all[b1], norm_all[b2]], axis=1)

    @pl.loop(0, STEPS // 2)
    def _(i):
        found = jnp.zeros((8, WIDTH), jnp.float32)
        for u in range(2):
            found = found + jnp.where(slot_masks(i, u) > 0.0, norm_row(2 * i + u), 0.0)
        slot_norm = jnp.sum(found, axis=1, keepdims=True)
        live = slot_i[pl.ds(8 * i, 8), :] >= 0
        coefficient = jnp.exp2(slot_pos[pl.ds(8 * i, 8), :] - slot_norm) - 1.0
        slot_c[pl.ds(8 * i, 8), :] = jnp.where(live, LOGIT_SCALE * coefficient, 0.0)

    cx[group] = jnp.transpose(slot_c[...])[0:8, :]
    c_copy = pair_copy(cx.at[group], cx.at[group], 2)
    c_copy.start()

    copies = [up_copy, r_copy, c_copy]
    half = NEGS // 2
    for h in range(2):
        part = slice(half * h, half * (h + 1))
        acc[...] = jnp.zeros_like(acc)

        @pl.loop(0, STEPS // 4)
        def _(g):
            probs, rows = [], []
            for u in range(4):
                t = 4 * g + u
                probs.append(
                    jnp.exp2(scores[t, part, :] - norm_row(t)).astype(jnp.bfloat16)
                )
                rows.append(two_blocks(t))
            acc[...] += jnp.dot(
                jnp.concatenate(probs, axis=1), jnp.concatenate(rows, axis=0),
                preferred_element_type=jnp.float32,
            )

        gsend[h] = acc[...].astype(gsend.dtype)
        g_copy = pair_copy(gsend.at[h], grecv.at[h], 3 + h)
        g_copy.start()
        copies.append(g_copy)

    for copy in copies:
        copy.wait()
    for h in range(2):
        part = slice(half * h, half * (h + 1))
        gsum_ref[part, :] = gsend[h].astype(jnp.float32) + grecv[h].astype(jnp.float32)
    for k in range(2):
        up_out[SLOTS * k : SLOTS * (k + 1), :] = upx[k]
        r_out[:, SLOTS * k : SLOTS * (k + 1)] = rx[k]
        c_out[:, SLOTS * k : SLOTS * (k + 1)] = cx[k]
    wait_bytes(users.at[pl.ds(0, BLOCKS - 1)], send_sem)
    wait_bytes(ids_all.at[pl.ds(0, BLOCKS - 1)], ids_send)
    wait_bytes(stat_in.at[pl.ds(0, BLOCKS - 1)], stat_send)
    wait_bytes(norm_all.at[pl.ds(0, BLOCKS - 1)], norm_send)


def head(u, ids, negr, lp, table):
    f32, bf16, i32 = jnp.float32, jnp.bfloat16, jnp.int32
    vmem = pl.BlockSpec(memory_space=pltpu.VMEM)
    dma = pltpu.SemaphoreType.DMA
    V = pltpu.VMEM
    return pl.pallas_call(
        head_kernel,
        out_shape=(
            jax.ShapeDtypeStruct((NEGS, WIDTH), f32),
            jax.ShapeDtypeStruct((2 * SLOTS, WIDTH), bf16),
            jax.ShapeDtypeStruct((8, 2 * SLOTS), i32),
            jax.ShapeDtypeStruct((8, 2 * SLOTS), f32),
            jax.ShapeDtypeStruct((1, ROWS), f32),
        ),
        in_specs=[vmem, vmem, vmem, vmem, pl.BlockSpec(memory_space=pl.ANY)],
        out_specs=(vmem,) * 5,
        scratch_shapes=[
            V((BLOCKS, ROWS, WIDTH), bf16),
            V((STEPS, NEGS, 2 * ROWS), f32),
            V((NEGS, WIDTH), bf16),
            V((NEGS, 128), f32),
            V((ITEMS, WIDTH), f32),
            V((ITEMS, WIDTH), bf16),
            V((BLOCKS, 1, ROWS), i32),
            V((BLOCKS, ROWS), i32),
            V((BLOCKS, ROWS), i32),
            V((BLOCKS, ROWS), i32),
            V((BLOCKS, ROWS), i32),
            V((SLOTS, 128), i32),
            V((SLOTS, 128), i32),
            V((SLOTS, WIDTH), f32),
            V((SLOTS, 128), f32),
            V((SLOTS, 128), f32),
            V((SLOTS, WIDTH), f32),
            V((SLOTS, 128), f32),
            V((BLOCKS, 2, ROWS), f32),
            V((BLOCKS, 2, ROWS), f32),
            V((BLOCKS, 1, ROWS), f32),
            V((NEGS // 2, WIDTH), f32),
            V((2, NEGS // 2, WIDTH), bf16),
            V((2, NEGS // 2, WIDTH), bf16),
            V((2, SLOTS, WIDTH), bf16),
            V((2, 8, SLOTS), i32),
            V((2, 8, SLOTS), f32),
            dma((BLOCKS,)),
            dma, dma, dma, dma, dma, dma, dma, dma,
            dma((5,)),
            dma((5,)),
        ],
        compiler_params=pltpu.CompilerParams(
            has_side_effects=True, vmem_limit_bytes=58 * 1024 * 1024
        ),
        cost_estimate=pl.CostEstimate(
            flops=3 * 2 * 16384 * NEGS * WIDTH, bytes_accessed=4 << 20,
            transcendentals=2 * 16384 * NEGS,
        ),
        name="sampled_head",
    )(u, ids, negr, lp, table)


TILE = 256


def update_kernel(
    negr_ref, r_ref, c_ref, gsum_ref, up_ref, table_ref, accum_ref,
    new_table_ref, new_accum_ref, g_hi, g_lo,
):
    @pl.when(pl.program_id(0) == 0)
    def _():
        g = LOGIT_SCALE * gsum_ref[...]
        top = g.astype(jnp.bfloat16)
        g_hi[...] = top
        g_lo[...] = (g - top.astype(jnp.float32)).astype(jnp.bfloat16)

    row = lax.broadcasted_iota(jnp.int32, (TILE, NEGS), 0) + TILE * pl.program_id(0)
    hot = jnp.where(row == negr_ref[...], 1.0, 0.0).astype(jnp.bfloat16)
    weight = jnp.where(row == r_ref[0:1, :], c_ref[0:1, :], 0.0)
    w_hi = weight.astype(jnp.bfloat16)
    w_lo = (weight - w_hi.astype(jnp.float32)).astype(jnp.bfloat16)

    def mm(a, b):
        return jnp.dot(a, b, preferred_element_type=jnp.float32)

    grad = (mm(hot, g_hi[...]) + mm(hot, g_lo[...])) + (
        mm(w_hi, up_ref[...]) + mm(w_lo, up_ref[...])
    )
    accum = accum_ref[...] + grad * grad
    new_accum_ref[...] = accum
    new_table_ref[...] = table_ref[...] - STEP_RATE * grad * lax.rsqrt(accum)


def update(negr, rows, coefs, gsum, ups, table, accum):
    whole = lambda shape: pl.BlockSpec(shape, lambda i: (0, 0))
    tile = pl.BlockSpec((TILE, WIDTH), lambda i: (i, 0))
    return pl.pallas_call(
        update_kernel,
        grid=(ITEMS // TILE,),
        out_shape=(jax.ShapeDtypeStruct((ITEMS, WIDTH), jnp.float32),) * 2,
        in_specs=[
            whole((1, NEGS)), whole((8, 2 * SLOTS)), whole((8, 2 * SLOTS)),
            whole((NEGS, WIDTH)), whole((2 * SLOTS, WIDTH)), tile, tile,
        ],
        out_specs=(tile, tile),
        scratch_shapes=[pltpu.VMEM((NEGS, WIDTH), jnp.bfloat16)] * 2,
        compiler_params=pltpu.CompilerParams(vmem_limit_bytes=16 * 1024 * 1024),
        name="table_update",
    )(negr, rows, coefs, gsum, ups, table, accum)


def per_device(
    user_vectors, item_table, grad_accum, log_prob, positive_shard, positive_row, negatives
):
    ids = positive_shard.reshape(1, ROWS) * ITEMS + positive_row.reshape(1, ROWS)
    negr = negatives.reshape(1, NEGS)
    gsum, ups, rows, coefs, loss = head(
        user_vectors, ids, negr, log_prob.reshape(1, ITEMS), item_table
    )
    new_table, new_accum = update(negr, rows, coefs, gsum, ups, item_table, grad_accum)
    return (new_table, new_accum, loss.reshape(ROWS))


def solution(mesh):
    in_specs = (
        P(("item", "batch"), None),
        P("item", None),
        P("item", None),
        P("item"),
        P(("item", "batch"), None),
        P(("item", "batch")),
        P("item"),
    )
    out_specs = (P("item", None), P("item", None), P(("item", "batch")))
    return jax.shard_map(
        per_device, mesh=mesh, in_specs=in_specs, out_specs=out_specs, check_vma=False
    )
```

```python
import math

import jax
import jax.numpy as jnp
from jax import lax
from jax.experimental import pallas as pl
from jax.experimental.pallas import tpu as pltpu
from jax.sharding import PartitionSpec as P

LOGIT_SCALE = 2.5
STEP_RATE = 0.05
LOG2E = math.log2(math.e)
LN2 = math.log(2.0)
FLOOR = -1e30

BLOCKS = 128
ROWS = 128
WIDTH = 256
ITEMS = 2048
NEGS = 512
STEPS = 64
SLOTS = 256


RING = (0, 1, 3, 2)


def order4(q):
    return jnp.where(q < 2, q, 5 - q)


def head_kernel(
    u_ref, shard_ref, row_ref, negr_ref, lp_ref, table_ref,
    gsum_ref, up_out, r_out, c_out, loss_ref,
    users, scores_own, scores_sib, negs, bias, tab, tabb, ids_all, slot_i, slot_r,
    slot_t, slot_lp, slot_pos, slot_u,
    stat_out, stat_in, norm_all, acc, gsend, grecv, upx, rx, cx,
    block_sem, send_sem, tab_sem, ids_sem, ids_send, stat_sem, stat_send, norm_sem, norm_send,
    pair_send, pair_recv,
):
    me = lax.axis_index("item")
    group = lax.axis_index("batch")
    other = 1 - group
    core = lax.rem(me, 2)
    sib = me + 1 - 2 * core
    x_pos = lax.rem(me // 2, 4)
    z_pos = lax.rem(me // 8, 4)
    y_pos = me // 32
    outer = jnp.where(core == 0, y_pos, x_pos)
    inner = jnp.where(core == 0, x_pos, y_pos)
    s_out = jnp.where(core == 0, 32, 2)
    s_in = 34 - s_out

    def place(do, di, dz):
        return (
            lax.rem(outer + do, 4) * s_out + lax.rem(inner + di, 4) * s_in
            + lax.rem(z_pos + dz, 4) * 8 + core
        )

    def sib_place(do, di, dz):
        return (
            lax.rem(inner + do, 4) * s_in + lax.rem(outer + di, 4) * s_out
            + lax.rem(z_pos + dz, 4) * 8 + 1 - core
        )

    barrier = pltpu.get_barrier_semaphore()
    pl.semaphore_signal(
        barrier, inc=1, device_id={"batch": other}, device_id_type=pl.DeviceIdType.MESH
    )

    @pl.loop(1, BLOCKS)
    def _(j):
        pl.semaphore_signal(
            barrier, inc=1, device_id={"item": lax.rem(me + j, BLOCKS)},
            device_id_type=pl.DeviceIdType.MESH,
        )

    table_copy = pltpu.make_async_copy(table_ref, tab, tab_sem)
    table_copy.start()
    users[me] = u_ref[...]
    ids_all[me] = shard_ref[...] * ITEMS + row_ref[...]
    pl.semaphore_wait(barrier, BLOCKS)

    def block_copy(b, dev):
        return pltpu.make_async_remote_copy(
            src_ref=users.at[b], dst_ref=users.at[b], send_sem=send_sem,
            recv_sem=block_sem.at[b], device_id={"item": dev},
            device_id_type=pl.DeviceIdType.MESH,
        )

    def arrived(b):
        block_copy(b, sib).wait_recv()

    def send(b, *devices):
        for dev in devices:
            block_copy(b, dev).start()

    out_up, out_down = place(1, 0, 0), place(3, 0, 0)
    in_up, in_down = place(0, 1, 0), place(0, 3, 0)
    z_up, z_down = place(0, 0, 1), place(0, 0, 3)

    def forward_plane(q):
        di, dz = RING[q // 4], RING[q % 4]
        b = place(0, di, dz)
        if q > 0:
            arrived(b)
        send(b, out_down, out_up)
        if di == 0:
            send(b, in_down, in_up)
            if dz == 0:
                send(b, z_down, z_up)
            if dz == 3:
                far = place(0, 0, 1 + 2 * core)
                send(far, jnp.where(core == 0, z_down, z_up))
        if di == 1 and q % 2 == 0:
            send(b, in_down)
        if di == 3 and q % 2 == 1:
            send(b, in_up)
        send(b, sib)

    def peer_copy(src, dst, send_to, recv, dev):
        return pltpu.make_async_remote_copy(
            src_ref=src, dst_ref=dst, send_sem=send_to, recv_sem=recv,
            device_id={"item": dev}, device_id_type=pl.DeviceIdType.MESH,
        )

    def wait_bytes(ref, sem):
        pltpu.make_async_copy(ref, ref, sem).wait()

    forward_plane(0)

    @pl.loop(1, BLOCKS)
    def _(j):
        dev = lax.rem(me + j, BLOCKS)
        peer_copy(ids_all.at[me], ids_all.at[me], ids_send, ids_sem, dev).start()

    table_copy.wait()
    tabb[...] = tab[...].astype(jnp.bfloat16)
    lp2 = lp_ref[...] * LOG2E

    def gather(row_cols):
        lane = lax.broadcasted_iota(jnp.int32, row_cols.shape, 1)
        hots = [row_cols == lane + 128 * j for j in range(ITEMS // 128)]
        hot = jnp.concatenate([h.astype(jnp.float32).astype(jnp.bfloat16) for h in hots], axis=1)
        rows = jnp.dot(hot, tabb[...], preferred_element_type=jnp.float32)
        total = jnp.zeros(row_cols.shape, jnp.float32)
        for j, h in enumerate(hots):
            total = total + jnp.where(h, lp2[:, 128 * j : 128 * (j + 1)], 0.0)
        lp_rows = jnp.broadcast_to(jnp.sum(total, axis=1, keepdims=True), row_cols.shape)
        return rows, lp_rows

    neg_cols = jnp.transpose(jnp.broadcast_to(negr_ref[...], (128, NEGS)))
    for q in range(NEGS // 128):
        part = slice(128 * q, 128 * (q + 1))
        rows, lp_rows = gather(neg_cols[part])
        negs[part, :] = rows.astype(jnp.bfloat16)
        bias[part, :] = lp_rows

    for q in range(1, 16):
        forward_plane(q)

    wait_bytes(ids_all.at[pl.ds(0, BLOCKS - 1)], ids_sem)
    ids = ids_all[:, 0, :]
    wide = (BLOCKS, ROWS)
    lane = lax.broadcasted_iota(jnp.int32, wide, 1)
    mine = (ids // ITEMS) == me
    row = lax.rem(ids, ITEMS)
    lo = jnp.broadcast_to(
        jnp.min(jnp.where(mine, lane, ROWS), axis=1, keepdims=True), wide
    )
    hi = jnp.broadcast_to(jnp.max(jnp.where(mine, lane, -1), axis=1, keepdims=True), wide)
    first = mine & (lane == lo)
    last = mine & (lane == hi) & (hi > lo)
    slot_i[0:BLOCKS, :] = jnp.where(lo < ROWS, lo, -1)
    slot_i[BLOCKS:, :] = jnp.where(hi > lo, hi, -1)
    for c, hit in enumerate((first, last)):
        slot_r[BLOCKS * c : BLOCKS * (c + 1), :] = jnp.broadcast_to(
            jnp.max(jnp.where(hit, row, -1), axis=1, keepdims=True), wide
        )
    for q in range(SLOTS // 128):
        part = slice(128 * q, 128 * (q + 1))
        rows, lp_rows = gather(slot_r[part, :])
        slot_t[part, :] = rows
        slot_lp[part, :] = lp_rows

    sub = lax.broadcasted_iota(jnp.int32, (8, 128), 0)
    lane8 = lax.broadcasted_iota(jnp.int32, (8, 128), 1)

    def pick(values):
        out = jnp.broadcast_to(values[3], (8, values[3].shape[1]))
        s8 = lax.broadcasted_iota(jnp.int32, out.shape, 0)
        for c in (2, 1, 0):
            out = jnp.where(s8 == c, values[c], out)
        return out

    def tile_blocks(s):
        near = s - 8
        far = 2 * (s - 24)
        offsets = []
        for h in range(2):
            k = jnp.where(s < 8, 2 * s + h, jnp.where(s < 24, near, far + h))
            do = jnp.where(s < 8, 0, jnp.where(s < 24, 1 + 2 * h, 2))
            offsets.append((do, order4(k // 4), order4(lax.rem(k, 4))))
        return [place(*o) for o in offsets], [sib_place(*o) for o in offsets]

    def both_users(blocks):
        return jnp.concatenate([users[blocks[0]], users[blocks[1]]], axis=0)

    def score(blocks, scores):
        pair = both_users(blocks)
        a, b = blocks
        at = [a, BLOCKS + a, b, BLOCKS + b]
        index = [slot_i[pl.ds(r, 1), :] for r in at]
        left = jnp.where(sub == 0, index[0], jnp.where(sub == 1, index[1], -2)) == lane8
        right = jnp.where(sub == 2, index[2], jnp.where(sub == 3, index[3], -2)) == lane8
        mask = jnp.concatenate([jnp.where(left, 1.0, 0.0), jnp.where(right, 1.0, 0.0)], axis=1)
        hot = jnp.concatenate([mask, jnp.zeros_like(mask)], axis=0).astype(jnp.bfloat16)
        raw = lax.dot_general(
            negs[...], pair, (((1,), (1,)), ((), ())), preferred_element_type=jnp.float32
        )
        cols = bias[...]
        scaled = raw * (LOGIT_SCALE * LOG2E) - jnp.concatenate([cols, cols], axis=1)
        scores[a // 2] = scaled[:, :ROWS]
        scores[b // 2] = scaled[:, ROWS:]
        peak = jnp.max(scaled, axis=0, keepdims=True)
        gathered = jnp.dot(hot, pair, preferred_element_type=jnp.float32)[0:8]
        dots = jnp.sum(
            gathered * pick([slot_t[pl.ds(r, 1), :] for r in at]), axis=1, keepdims=True
        )
        pos = dots * (LOGIT_SCALE * LOG2E) - pick([slot_lp[pl.ds(r, 1), :] for r in at])
        for c, r in enumerate(at):
            slot_u[pl.ds(r, 1), :] = gathered[c : c + 1]
            slot_pos[pl.ds(r, 1), :] = pos[c : c + 1]
        pos_row = jnp.max(
            jnp.where(mask > 0.0, jnp.concatenate([pos, pos], axis=1), FLOOR),
            axis=0, keepdims=True,
        )
        return peak, pos_row

    def summed(blocks, scores, peak, pos_row):
        for h, b in enumerate(blocks):
            part = slice(ROWS * h, ROWS * (h + 1))
            total = jnp.sum(jnp.exp2(scores[b // 2] - peak[:, part]), axis=0, keepdims=True)
            lse = peak[:, part] + jnp.log(total) * LOG2E
            stat_out[b] = jnp.concatenate([lse, pos_row[:, part]], axis=0)

    def tile(s):
        own, sibs = tile_blocks(s)
        first_own = score(own, scores_own)
        first_sib = score(sibs, scores_sib)
        summed(own, scores_own, *first_own)
        summed(sibs, scores_sib, *first_sib)

    def send_stats(b):
        peer_copy(stat_out.at[b], stat_in.at[me], stat_send, stat_sem, b).start()

    def before_tile(s):
        @pl.when(s > 0)
        def _():
            own, sibs = tile_blocks(s - 1)

            @pl.when(s > 1)
            def _():
                send_stats(own[0])

            send_stats(own[1])
            send_stats(sibs[0])
            send_stats(sibs[1])

        for b in tile_blocks(s)[1]:
            arrived(b)

    @pl.loop(0, 8)
    def _(r):
        for h in range(2):
            k = 2 * r + h
            di, dz = order4(k // 4), order4(lax.rem(k, 4))
            b = place(1, di, dz)
            arrived(b)
            if h == 0:
                send(b, out_down)
            send(b, sib)
            b = place(3, di, dz)
            arrived(b)
            if h == 1:
                send(b, out_up)
            send(b, sib)
            before_tile(k)
            tile(k)

    @pl.loop(0, 8)
    def _(r):
        for h in range(2):
            k = 2 * r + h
            b = place(2, order4(k // 4), order4(lax.rem(k, 4)))
            arrived(b)
            send(b, sib)
        for h in range(2):
            before_tile(16 + 2 * r + h)
            tile(16 + 2 * r + h)

    own, sibs = tile_blocks(STEPS // 2 - 1)
    for b in own + sibs:
        send_stats(b)
    stat_in[me] = stat_out[me]

    def pair_copy(src, dst, k):
        return pltpu.make_async_remote_copy(
            src_ref=src, dst_ref=dst, send_sem=pair_send.at[k], recv_sem=pair_recv.at[k],
            device_id={"batch": other}, device_id_type=pl.DeviceIdType.MESH,
        )

    def to_lanes(cols):
        return jnp.concatenate(
            [jnp.transpose(cols[BLOCKS * c : BLOCKS * (c + 1)])[0:8, :] for c in range(2)], axis=1
        )

    wait_bytes(stat_in.at[pl.ds(0, BLOCKS - 1)], stat_sem)
    lses = stat_in[:, 0, :]
    pos_own = jnp.max(stat_in[:, 1, :], axis=0, keepdims=True)
    top = jnp.maximum(jnp.max(lses, axis=0, keepdims=True), pos_own)
    total = jnp.sum(jnp.exp2(lses - top), axis=0, keepdims=True) + jnp.exp2(pos_own - top)
    norm = top + jnp.log(total) * LOG2E
    norm_all[me] = norm

    @pl.loop(1, BLOCKS)
    def _(j):
        dev = lax.rem(me + j, BLOCKS)
        peer_copy(norm_all.at[me], norm_all.at[me], norm_send, norm_sem, dev).start()

    loss_ref[...] = (norm - pos_own) * LN2
    upx[group] = slot_u[...].astype(jnp.bfloat16)
    rx[group] = to_lanes(slot_r[...])
    up_copy = pair_copy(upx.at[group], upx.at[group], 0)
    r_copy = pair_copy(rx.at[group], rx.at[group], 1)
    up_copy.start()
    r_copy.start()
    wait_bytes(norm_all.at[pl.ds(0, BLOCKS - 1)], norm_sem)

    norms = norm_all[:, 0, :]
    lane = lax.broadcasted_iota(jnp.int32, wide, 1)
    coefs = []
    for c in range(2):
        part = slice(BLOCKS * c, BLOCKS * (c + 1))
        index = slot_i[part, :]
        found = jnp.sum(jnp.where(index == lane, norms, 0.0), axis=1, keepdims=True)
        coefficient = jnp.exp2(slot_pos[part, :] - found) - 1.0
        coefs.append(jnp.where(index >= 0, LOGIT_SCALE * coefficient, 0.0))
    cx[group] = to_lanes(jnp.concatenate(coefs, axis=0))
    c_copy = pair_copy(cx.at[group], cx.at[group], 2)
    c_copy.start()

    copies = [up_copy, r_copy, c_copy]
    half = NEGS // 2
    for h in range(2):
        part = slice(half * h, half * (h + 1))
        acc[...] = jnp.zeros_like(acc)

        @pl.loop(0, STEPS // 8)
        def _(g):
            probs, rows = [], []
            for u in range(8):
                c = 8 * g + u
                for scores, b in ((scores_own, 2 * c + core), (scores_sib, 2 * c + 1 - core)):
                    probs.append(
                        jnp.exp2(scores[c, part, :] - norm_all[b]).astype(jnp.bfloat16)
                    )
                    rows.append(users[b])
            acc[...] += jnp.dot(
                jnp.concatenate(probs, axis=1), jnp.concatenate(rows, axis=0),
                preferred_element_type=jnp.float32,
            )

        gsend[h] = acc[...].astype(gsend.dtype)
        g_copy = pair_copy(gsend.at[h], grecv.at[h], 3 + h)
        g_copy.start()
        copies.append(g_copy)

    for copy in copies:
        copy.wait()
    for h in range(2):
        part = slice(half * h, half * (h + 1))
        gsum_ref[part, :] = gsend[h].astype(jnp.float32) + grecv[h].astype(jnp.float32)
    for k in range(2):
        up_out[SLOTS * k : SLOTS * (k + 1), :] = upx[k]
        r_out[:, SLOTS * k : SLOTS * (k + 1)] = rx[k]
        c_out[:, SLOTS * k : SLOTS * (k + 1)] = cx[k]
    wait_bytes(users.at[pl.ds(0, BLOCKS - 1)], send_sem)
    wait_bytes(ids_all.at[pl.ds(0, BLOCKS - 1)], ids_send)
    wait_bytes(stat_in.at[pl.ds(0, BLOCKS - 1)], stat_send)
    wait_bytes(norm_all.at[pl.ds(0, BLOCKS - 1)], norm_send)


def head(u, shards, rows, negr, lp, table):
    f32, bf16, i32 = jnp.float32, jnp.bfloat16, jnp.int32
    vmem = pl.BlockSpec(memory_space=pltpu.VMEM)
    dma = pltpu.SemaphoreType.DMA
    V = pltpu.VMEM
    return pl.pallas_call(
        head_kernel,
        out_shape=(
            jax.ShapeDtypeStruct((NEGS, WIDTH), f32),
            jax.ShapeDtypeStruct((2 * SLOTS, WIDTH), bf16),
            jax.ShapeDtypeStruct((8, 2 * SLOTS), i32),
            jax.ShapeDtypeStruct((8, 2 * SLOTS), f32),
            jax.ShapeDtypeStruct((1, ROWS), f32),
        ),
        in_specs=[vmem] * 5 + [pl.BlockSpec(memory_space=pl.ANY)],
        out_specs=(vmem,) * 5,
        scratch_shapes=[
            V((BLOCKS, ROWS, WIDTH), bf16),
            V((STEPS, NEGS, ROWS), f32),
            V((STEPS, NEGS, ROWS), f32),
            V((NEGS, WIDTH), bf16),
            V((NEGS, 128), f32),
            V((ITEMS, WIDTH), f32),
            V((ITEMS, WIDTH), bf16),
            V((BLOCKS, 1, ROWS), i32),
            V((SLOTS, 128), i32),
            V((SLOTS, 128), i32),
            V((SLOTS, WIDTH), f32),
            V((SLOTS, 128), f32),
            V((SLOTS, 128), f32),
            V((SLOTS, WIDTH), f32),
            V((BLOCKS, 2, ROWS), f32),
            V((BLOCKS, 2, ROWS), f32),
            V((BLOCKS, 1, ROWS), f32),
            V((NEGS // 2, WIDTH), f32),
            V((2, NEGS // 2, WIDTH), bf16),
            V((2, NEGS // 2, WIDTH), bf16),
            V((2, SLOTS, WIDTH), bf16),
            V((2, 8, SLOTS), i32),
            V((2, 8, SLOTS), f32),
            dma((BLOCKS,)),
            dma, dma, dma, dma, dma, dma, dma, dma,
            dma((5,)),
            dma((5,)),
        ],
        compiler_params=pltpu.CompilerParams(
            has_side_effects=True, vmem_limit_bytes=58 * 1024 * 1024, collective_id=0
        ),
        cost_estimate=pl.CostEstimate(
            flops=3 * 2 * 16384 * NEGS * WIDTH, bytes_accessed=4 << 20,
            transcendentals=2 * 16384 * NEGS,
        ),
        name="sampled_head",
    )(u, shards, rows, negr, lp, table)


TILE = 512


def update_kernel(
    negr_ref, r_ref, c_ref, gsum_ref, up_ref, table_ref, accum_ref,
    new_table_ref, new_accum_ref, g_hi, g_lo,
):
    @pl.when(pl.program_id(0) == 0)
    def _():
        g = LOGIT_SCALE * gsum_ref[...]
        top = g.astype(jnp.bfloat16)
        g_hi[...] = top
        g_lo[...] = (g - top.astype(jnp.float32)).astype(jnp.bfloat16)

    row = lax.broadcasted_iota(jnp.int32, (TILE, NEGS), 0) + TILE * pl.program_id(0)
    hot = jnp.where(row == negr_ref[...], 1.0, 0.0).astype(jnp.bfloat16)
    weight = jnp.where(row == r_ref[0:1, :], c_ref[0:1, :], 0.0)
    w_hi = weight.astype(jnp.bfloat16)
    w_lo = (weight - w_hi.astype(jnp.float32)).astype(jnp.bfloat16)

    def mm(a, b):
        return jnp.dot(a, b, preferred_element_type=jnp.float32)

    grad = (mm(hot, g_hi[...]) + mm(hot, g_lo[...])) + (
        mm(w_hi, up_ref[...]) + mm(w_lo, up_ref[...])
    )
    accum = accum_ref[...] + grad * grad
    new_accum_ref[...] = accum
    new_table_ref[...] = table_ref[...] - STEP_RATE * grad * lax.rsqrt(accum)


def update(negr, rows, coefs, gsum, ups, table, accum):
    whole = lambda shape: pl.BlockSpec(shape, lambda i: (0, 0))
    tile = pl.BlockSpec((TILE, WIDTH), lambda i: (i, 0))
    return pl.pallas_call(
        update_kernel,
        grid=(ITEMS // TILE,),
        out_shape=(jax.ShapeDtypeStruct((ITEMS, WIDTH), jnp.float32),) * 2,
        in_specs=[
            whole((1, NEGS)), whole((8, 2 * SLOTS)), whole((8, 2 * SLOTS)),
            whole((NEGS, WIDTH)), whole((2 * SLOTS, WIDTH)), tile, tile,
        ],
        out_specs=(tile, tile),
        scratch_shapes=[pltpu.VMEM((NEGS, WIDTH), jnp.bfloat16)] * 2,
        compiler_params=pltpu.CompilerParams(vmem_limit_bytes=60 * 1024 * 1024),
        name="table_update",
    )(negr, rows, coefs, gsum, ups, table, accum)


def per_device(
    user_vectors, item_table, grad_accum, log_prob, positive_shard, positive_row, negatives
):
    negr = negatives.reshape(1, NEGS)
    gsum, ups, rows, coefs, loss = head(
        user_vectors, positive_shard.reshape(1, ROWS), positive_row.reshape(1, ROWS), negr,
        log_prob.reshape(1, ITEMS), item_table,
    )
    new_table, new_accum = update(negr, rows, coefs, gsum, ups, item_table, grad_accum)
    return (new_table, new_accum, loss.reshape(ROWS))


def solution(mesh):
    in_specs = (
        P(("item", "batch"), None),
        P("item", None),
        P("item", None),
        P("item"),
        P(("item", "batch"), None),
        P(("item", "batch")),
        P("item"),
    )
    out_specs = (P("item", None), P("item", None), P(("item", "batch")))
    return jax.shard_map(
        per_device, mesh=mesh, in_specs=in_specs, out_specs=out_specs, check_vma=False
    )
```

```python
import math

import jax
import jax.numpy as jnp
from jax import lax
from jax.experimental import pallas as pl
from jax.experimental.pallas import tpu as pltpu
from jax.sharding import PartitionSpec as P

LOGIT_SCALE = 2.5
STEP_RATE = 0.05
LOG2E = math.log2(math.e)
LN2 = math.log(2.0)
FLOOR = -1e30

BLOCKS = 128
ROWS = 128
WIDTH = 256
ITEMS = 2048
NEGS = 512
STEPS = 64
AHEAD = 1
SLOTS = 256


RING = (0, 1, 3, 2)


def order4(q):
    return jnp.where(q < 2, q, 5 - q)


def head_kernel(
    u_ref, shard_ref, row_ref, negr_ref, lp_ref, table_ref,
    gsum_ref, up_out, r_out, c_out, loss_ref,
    users, scores_own, scores_sib, negs, bias, tab, tabb, ids_all, slot_i, slot_r,
    slot_t, slot_lp, slot_pos, slot_u,
    stat_out, stat_in, norm_all, acc, gsend, grecv, upx, rx, cx,
    block_sem, send_sem, tab_sem, ids_sem, ids_send, stat_sem, stat_send, norm_sem, norm_send,
    pair_send, pair_recv,
):
    me = lax.axis_index("item")
    group = lax.axis_index("batch")
    other = 1 - group
    core = lax.rem(me, 2)
    sib = me + 1 - 2 * core
    x_pos = lax.rem(me // 2, 4)
    z_pos = lax.rem(me // 8, 4)
    y_pos = me // 32
    outer = jnp.where(core == 0, y_pos, x_pos)
    inner = jnp.where(core == 0, x_pos, y_pos)
    s_out = jnp.where(core == 0, 32, 2)
    s_in = 34 - s_out

    def place(do, di, dz):
        return (
            lax.rem(outer + do, 4) * s_out + lax.rem(inner + di, 4) * s_in
            + lax.rem(z_pos + dz, 4) * 8 + core
        )

    def sib_place(do, di, dz):
        return (
            lax.rem(inner + do, 4) * s_in + lax.rem(outer + di, 4) * s_out
            + lax.rem(z_pos + dz, 4) * 8 + 1 - core
        )

    barrier = pltpu.get_barrier_semaphore()
    pl.semaphore_signal(
        barrier, inc=1, device_id={"batch": other}, device_id_type=pl.DeviceIdType.MESH
    )

    @pl.loop(1, BLOCKS)
    def _(j):
        pl.semaphore_signal(
            barrier, inc=1, device_id={"item": lax.rem(me + j, BLOCKS)},
            device_id_type=pl.DeviceIdType.MESH,
        )

    table_copy = pltpu.make_async_copy(table_ref, tab, tab_sem)
    table_copy.start()
    users[me] = u_ref[...]
    ids_all[me] = shard_ref[...] * ITEMS + row_ref[...]
    pl.semaphore_wait(barrier, BLOCKS)

    def block_copy(b, dev):
        return pltpu.make_async_remote_copy(
            src_ref=users.at[b], dst_ref=users.at[b], send_sem=send_sem,
            recv_sem=block_sem.at[b], device_id={"item": dev},
            device_id_type=pl.DeviceIdType.MESH,
        )

    def arrived(b):
        block_copy(b, sib).wait_recv()

    def send(b, *devices):
        for dev in devices:
            block_copy(b, dev).start()

    out_up, out_down = place(1, 0, 0), place(3, 0, 0)
    in_up, in_down = place(0, 1, 0), place(0, 3, 0)
    z_up, z_down = place(0, 0, 1), place(0, 0, 3)

    def plane_block(ki, j):
        dz = RING[j]
        b = place(0, order4(ki), dz)
        if j == 0:

            @pl.when(ki > 0)
            def _():
                arrived(b)
        else:
            arrived(b)

        @pl.when(ki == 0)
        def _():
            if j == 0:
                send(b, z_down, z_up)
            if j == 2:
                far = place(0, 0, 1 + 2 * core)
                send(far, jnp.where(core == 0, z_down, z_up))
            send(b, in_down, in_up)

        send(b, out_down, out_up)

        @pl.when(ki == (1 if j % 2 == 0 else 2))
        def _():
            send(b, in_down if j % 2 == 0 else in_up)

        send(b, sib)

    def peer_copy(src, dst, send_to, recv, dev):
        return pltpu.make_async_remote_copy(
            src_ref=src, dst_ref=dst, send_sem=send_to, recv_sem=recv,
            device_id={"item": dev}, device_id_type=pl.DeviceIdType.MESH,
        )

    def wait_bytes(ref, sem):
        pltpu.make_async_copy(ref, ref, sem).wait()

    plane_block(jnp.int32(0), 0)

    @pl.loop(1, BLOCKS)
    def _(j):
        dev = lax.rem(me + j, BLOCKS)
        peer_copy(ids_all.at[me], ids_all.at[me], ids_send, ids_sem, dev).start()

    table_copy.wait()
    tabb[...] = tab[...].astype(jnp.bfloat16)
    lp2 = lp_ref[...] * LOG2E

    def gather(row_cols):
        lane = lax.broadcasted_iota(jnp.int32, row_cols.shape, 1)
        hots = [row_cols == lane + 128 * j for j in range(ITEMS // 128)]
        hot = jnp.concatenate([h.astype(jnp.float32).astype(jnp.bfloat16) for h in hots], axis=1)
        rows = jnp.dot(hot, tabb[...], preferred_element_type=jnp.float32)
        total = jnp.zeros(row_cols.shape, jnp.float32)
        for j, h in enumerate(hots):
            total = total + jnp.where(h, lp2[:, 128 * j : 128 * (j + 1)], 0.0)
        lp_rows = jnp.broadcast_to(jnp.sum(total, axis=1, keepdims=True), row_cols.shape)
        return rows, lp_rows

    neg_cols = jnp.transpose(jnp.broadcast_to(negr_ref[...], (128, NEGS)))
    for q in range(NEGS // 128):
        part = slice(128 * q, 128 * (q + 1))
        rows, lp_rows = gather(neg_cols[part])
        negs[part, :] = rows.astype(jnp.bfloat16)
        bias[part, :] = lp_rows

    for q in range(1, 4 * AHEAD):
        plane_block(jnp.int32(q // 4), q % 4)

    wait_bytes(ids_all.at[pl.ds(0, BLOCKS - 1)], ids_sem)
    ids = ids_all[:, 0, :]
    wide = (BLOCKS, ROWS)
    lane = lax.broadcasted_iota(jnp.int32, wide, 1)
    mine = (ids // ITEMS) == me
    row = lax.rem(ids, ITEMS)
    lo = jnp.broadcast_to(
        jnp.min(jnp.where(mine, lane, ROWS), axis=1, keepdims=True), wide
    )
    hi = jnp.broadcast_to(jnp.max(jnp.where(mine, lane, -1), axis=1, keepdims=True), wide)
    first = mine & (lane == lo)
    last = mine & (lane == hi) & (hi > lo)
    slot_i[0:BLOCKS, :] = jnp.where(lo < ROWS, lo, -1)
    slot_i[BLOCKS:, :] = jnp.where(hi > lo, hi, -1)
    for c, hit in enumerate((first, last)):
        slot_r[BLOCKS * c : BLOCKS * (c + 1), :] = jnp.broadcast_to(
            jnp.max(jnp.where(hit, row, -1), axis=1, keepdims=True), wide
        )
    for q in range(SLOTS // 128):
        part = slice(128 * q, 128 * (q + 1))
        rows, lp_rows = gather(slot_r[part, :])
        slot_t[part, :] = rows
        slot_lp[part, :] = lp_rows

    sub = lax.broadcasted_iota(jnp.int32, (8, 128), 0)
    lane8 = lax.broadcasted_iota(jnp.int32, (8, 128), 1)

    def pick(values):
        out = jnp.broadcast_to(values[3], (8, values[3].shape[1]))
        s8 = lax.broadcasted_iota(jnp.int32, out.shape, 0)
        for c in (2, 1, 0):
            out = jnp.where(s8 == c, values[c], out)
        return out

    def tile_blocks(s):
        near = s - 8
        far = 2 * (s - 24)
        offsets = []
        for h in range(2):
            k = jnp.where(s < 8, 2 * s + h, jnp.where(s < 24, near, far + h))
            do = jnp.where(s < 8, 0, jnp.where(s < 24, 1 + 2 * h, 2))
            offsets.append((do, order4(k // 4), order4(lax.rem(k, 4))))
        return [place(*o) for o in offsets], [sib_place(*o) for o in offsets]

    def both_users(blocks):
        return jnp.concatenate([users[blocks[0]], users[blocks[1]]], axis=0)

    def score(blocks, scores):
        pair = both_users(blocks)
        a, b = blocks
        at = [a, BLOCKS + a, b, BLOCKS + b]
        index = [slot_i[pl.ds(r, 1), :] for r in at]
        left = jnp.where(sub == 0, index[0], jnp.where(sub == 1, index[1], -2)) == lane8
        right = jnp.where(sub == 2, index[2], jnp.where(sub == 3, index[3], -2)) == lane8
        mask = jnp.concatenate([jnp.where(left, 1.0, 0.0), jnp.where(right, 1.0, 0.0)], axis=1)
        hot = jnp.concatenate([mask, jnp.zeros_like(mask)], axis=0).astype(jnp.bfloat16)
        raw = lax.dot_general(
            negs[...], pair, (((1,), (1,)), ((), ())), preferred_element_type=jnp.float32
        )
        cols = bias[...]
        scaled = raw * (LOGIT_SCALE * LOG2E) - jnp.concatenate([cols, cols], axis=1)
        scores[a // 2] = scaled[:, :ROWS]
        scores[b // 2] = scaled[:, ROWS:]
        peak = jnp.max(scaled, axis=0, keepdims=True)
        gathered = jnp.dot(hot, pair, preferred_element_type=jnp.float32)[0:8]
        dots = jnp.sum(
            gathered * pick([slot_t[pl.ds(r, 1), :] for r in at]), axis=1, keepdims=True
        )
        pos = dots * (LOGIT_SCALE * LOG2E) - pick([slot_lp[pl.ds(r, 1), :] for r in at])
        for c, r in enumerate(at):
            slot_u[pl.ds(r, 1), :] = gathered[c : c + 1]
            slot_pos[pl.ds(r, 1), :] = pos[c : c + 1]
        pos_row = jnp.max(
            jnp.where(mask > 0.0, jnp.concatenate([pos, pos], axis=1), FLOOR),
            axis=0, keepdims=True,
        )
        return peak, pos_row

    def summed(blocks, scores, peak, pos_row):
        for h, b in enumerate(blocks):
            part = slice(ROWS * h, ROWS * (h + 1))
            total = jnp.sum(jnp.exp2(scores[b // 2] - peak[:, part]), axis=0, keepdims=True)
            lse = peak[:, part] + jnp.log(total) * LOG2E
            stat_out[b] = jnp.concatenate([lse, pos_row[:, part]], axis=0)

    def send_stats(b):
        peer_copy(stat_out.at[b], stat_in.at[me], stat_send, stat_sem, b).start()

    def tile(s):
        own, sibs = tile_blocks(s)
        for b in sibs:
            arrived(b)
        first_own = score(own, scores_own)
        first_sib = score(sibs, scores_sib)
        summed(own, scores_own, *first_own)
        summed(sibs, scores_sib, *first_sib)

        @pl.when(s > 0)
        def _():
            send_stats(own[0])

        send_stats(own[1])
        send_stats(sibs[0])
        send_stats(sibs[1])

    def far_block(ki, j):
        b = place(2, order4(ki), RING[j])
        arrived(b)
        send(b, sib)

    @pl.loop(0, 4)
    def _(m):
        for j in range(4):

            @pl.when(m < 4 - AHEAD)
            def _():
                plane_block(m + AHEAD, j)

            di, dz = order4(m), RING[j]
            b1, b3 = place(1, di, dz), place(3, di, dz)
            arrived(b1)
            if j % 2 == 0:
                send(b1, out_down)
            send(b1, sib)
            arrived(b3)
            if j % 2 == 1:
                send(b3, out_up)
            send(b3, sib)

            @pl.when(m > 0)
            def _():
                far_block(m - 1, j)

            k = 4 * m + j
            rest = 24 + (k - 6) // 2 if j % 2 == 0 else (k - 1) // 2

            @pl.loop(0, 2)
            def _(e):
                s = jnp.where(e == 0, k + 6, rest)

                @pl.when(k >= jnp.where(e == 0, 2, 6 if j % 2 == 0 else 0))
                def _():
                    tile(s)

    for j in range(4):
        far_block(3, j)

    @pl.loop(0, 5)
    def _(e):
        tile(jnp.where(e < 2, 22 + e, 27 + e))

    stat_in[me] = stat_out[me]

    def pair_copy(src, dst, k):
        return pltpu.make_async_remote_copy(
            src_ref=src, dst_ref=dst, send_sem=pair_send.at[k], recv_sem=pair_recv.at[k],
            device_id={"batch": other}, device_id_type=pl.DeviceIdType.MESH,
        )

    def to_lanes(cols):
        return jnp.concatenate(
            [jnp.transpose(cols[BLOCKS * c : BLOCKS * (c + 1)])[0:8, :] for c in range(2)], axis=1
        )

    wait_bytes(stat_in.at[pl.ds(0, BLOCKS - 1)], stat_sem)
    lses = stat_in[:, 0, :]
    pos_own = jnp.max(stat_in[:, 1, :], axis=0, keepdims=True)
    top = jnp.maximum(jnp.max(lses, axis=0, keepdims=True), pos_own)
    total = jnp.sum(jnp.exp2(lses - top), axis=0, keepdims=True) + jnp.exp2(pos_own - top)
    norm = top + jnp.log(total) * LOG2E
    norm_all[me] = norm

    @pl.loop(1, BLOCKS)
    def _(j):
        dev = lax.rem(me + j, BLOCKS)
        peer_copy(norm_all.at[me], norm_all.at[me], norm_send, norm_sem, dev).start()

    loss_ref[...] = (norm - pos_own) * LN2
    upx[group] = slot_u[...].astype(jnp.bfloat16)
    rx[group] = to_lanes(slot_r[...])
    up_copy = pair_copy(upx.at[group], upx.at[group], 0)
    r_copy = pair_copy(rx.at[group], rx.at[group], 1)
    up_copy.start()
    r_copy.start()
    wait_bytes(norm_all.at[pl.ds(0, BLOCKS - 1)], norm_sem)

    norms = norm_all[:, 0, :]
    lane = lax.broadcasted_iota(jnp.int32, wide, 1)
    coefs = []
    for c in range(2):
        part = slice(BLOCKS * c, BLOCKS * (c + 1))
        index = slot_i[part, :]
        found = jnp.sum(jnp.where(index == lane, norms, 0.0), axis=1, keepdims=True)
        coefficient = jnp.exp2(slot_pos[part, :] - found) - 1.0
        coefs.append(jnp.where(index >= 0, LOGIT_SCALE * coefficient, 0.0))
    cx[group] = to_lanes(jnp.concatenate(coefs, axis=0))
    c_copy = pair_copy(cx.at[group], cx.at[group], 2)
    c_copy.start()

    copies = [up_copy, r_copy, c_copy]
    half = NEGS // 2
    for h in range(2):
        part = slice(half * h, half * (h + 1))
        acc[...] = jnp.zeros_like(acc)

        @pl.loop(0, STEPS // 8)
        def _(g):
            probs, rows = [], []
            for u in range(8):
                c = 8 * g + u
                for scores, b in ((scores_own, 2 * c + core), (scores_sib, 2 * c + 1 - core)):
                    probs.append(
                        jnp.exp2(scores[c, part, :] - norm_all[b]).astype(jnp.bfloat16)
                    )
                    rows.append(users[b])
            acc[...] += jnp.dot(
                jnp.concatenate(probs, axis=1), jnp.concatenate(rows, axis=0),
                preferred_element_type=jnp.float32,
            )

        gsend[h] = acc[...].astype(gsend.dtype)
        g_copy = pair_copy(gsend.at[h], grecv.at[h], 3 + h)
        g_copy.start()
        copies.append(g_copy)

    for copy in copies:
        copy.wait()
    for h in range(2):
        part = slice(half * h, half * (h + 1))
        gsum_ref[part, :] = gsend[h].astype(jnp.float32) + grecv[h].astype(jnp.float32)
    for k in range(2):
        up_out[SLOTS * k : SLOTS * (k + 1), :] = upx[k]
        r_out[:, SLOTS * k : SLOTS * (k + 1)] = rx[k]
        c_out[:, SLOTS * k : SLOTS * (k + 1)] = cx[k]
    wait_bytes(users.at[pl.ds(0, BLOCKS - 1)], send_sem)
    wait_bytes(ids_all.at[pl.ds(0, BLOCKS - 1)], ids_send)
    wait_bytes(stat_in.at[pl.ds(0, BLOCKS - 1)], stat_send)
    wait_bytes(norm_all.at[pl.ds(0, BLOCKS - 1)], norm_send)


def head(u, shards, rows, negr, lp, table):
    f32, bf16, i32 = jnp.float32, jnp.bfloat16, jnp.int32
    vmem = pl.BlockSpec(memory_space=pltpu.VMEM)
    dma = pltpu.SemaphoreType.DMA
    V = pltpu.VMEM
    return pl.pallas_call(
        head_kernel,
        out_shape=(
            jax.ShapeDtypeStruct((NEGS, WIDTH), f32),
            jax.ShapeDtypeStruct((2 * SLOTS, WIDTH), bf16),
            jax.ShapeDtypeStruct((8, 2 * SLOTS), i32),
            jax.ShapeDtypeStruct((8, 2 * SLOTS), f32),
            jax.ShapeDtypeStruct((1, ROWS), f32),
        ),
        in_specs=[vmem] * 5 + [pl.BlockSpec(memory_space=pl.ANY)],
        out_specs=(vmem,) * 5,
        scratch_shapes=[
            V((BLOCKS, ROWS, WIDTH), bf16),
            V((STEPS, NEGS, ROWS), f32),
            V((STEPS, NEGS, ROWS), f32),
            V((NEGS, WIDTH), bf16),
            V((NEGS, 128), f32),
            V((ITEMS, WIDTH), f32),
            V((ITEMS, WIDTH), bf16),
            V((BLOCKS, 1, ROWS), i32),
            V((SLOTS, 128), i32),
            V((SLOTS, 128), i32),
            V((SLOTS, WIDTH), f32),
            V((SLOTS, 128), f32),
            V((SLOTS, 128), f32),
            V((SLOTS, WIDTH), f32),
            V((BLOCKS, 2, ROWS), f32),
            V((BLOCKS, 2, ROWS), f32),
            V((BLOCKS, 1, ROWS), f32),
            V((NEGS // 2, WIDTH), f32),
            V((2, NEGS // 2, WIDTH), bf16),
            V((2, NEGS // 2, WIDTH), bf16),
            V((2, SLOTS, WIDTH), bf16),
            V((2, 8, SLOTS), i32),
            V((2, 8, SLOTS), f32),
            dma((BLOCKS,)),
            dma, dma, dma, dma, dma, dma, dma, dma,
            dma((5,)),
            dma((5,)),
        ],
        compiler_params=pltpu.CompilerParams(
            has_side_effects=True, vmem_limit_bytes=58 * 1024 * 1024, collective_id=0
        ),
        cost_estimate=pl.CostEstimate(
            flops=3 * 2 * 16384 * NEGS * WIDTH, bytes_accessed=4 << 20,
            transcendentals=2 * 16384 * NEGS,
        ),
        name="sampled_head",
    )(u, shards, rows, negr, lp, table)


TILE = 512


def update_kernel(
    negr_ref, r_ref, c_ref, gsum_ref, up_ref, table_ref, accum_ref,
    new_table_ref, new_accum_ref, g_hi, g_lo,
):
    @pl.when(pl.program_id(0) == 0)
    def _():
        g = LOGIT_SCALE * gsum_ref[...]
        top = g.astype(jnp.bfloat16)
        g_hi[...] = top
        g_lo[...] = (g - top.astype(jnp.float32)).astype(jnp.bfloat16)

    row = lax.broadcasted_iota(jnp.int32, (TILE, NEGS), 0) + TILE * pl.program_id(0)
    hot = jnp.where(row == negr_ref[...], 1.0, 0.0).astype(jnp.bfloat16)
    weight = jnp.where(row == r_ref[0:1, :], c_ref[0:1, :], 0.0)
    w_hi = weight.astype(jnp.bfloat16)
    w_lo = (weight - w_hi.astype(jnp.float32)).astype(jnp.bfloat16)

    def mm(a, b):
        return jnp.dot(a, b, preferred_element_type=jnp.float32)

    grad = (mm(hot, g_hi[...]) + mm(hot, g_lo[...])) + (
        mm(w_hi, up_ref[...]) + mm(w_lo, up_ref[...])
    )
    accum = accum_ref[...] + grad * grad
    new_accum_ref[...] = accum
    new_table_ref[...] = table_ref[...] - STEP_RATE * grad * lax.rsqrt(accum)


def update(negr, rows, coefs, gsum, ups, table, accum):
    whole = lambda shape: pl.BlockSpec(shape, lambda i: (0, 0))
    tile = pl.BlockSpec((TILE, WIDTH), lambda i: (i, 0))
    return pl.pallas_call(
        update_kernel,
        grid=(ITEMS // TILE,),
        out_shape=(jax.ShapeDtypeStruct((ITEMS, WIDTH), jnp.float32),) * 2,
        in_specs=[
            whole((1, NEGS)), whole((8, 2 * SLOTS)), whole((8, 2 * SLOTS)),
            whole((NEGS, WIDTH)), whole((2 * SLOTS, WIDTH)), tile, tile,
        ],
        out_specs=(tile, tile),
        scratch_shapes=[pltpu.VMEM((NEGS, WIDTH), jnp.bfloat16)] * 2,
        compiler_params=pltpu.CompilerParams(vmem_limit_bytes=60 * 1024 * 1024),
        name="table_update",
    )(negr, rows, coefs, gsum, ups, table, accum)


def per_device(
    user_vectors, item_table, grad_accum, log_prob, positive_shard, positive_row, negatives
):
    negr = negatives.reshape(1, NEGS)
    gsum, ups, rows, coefs, loss = head(
        user_vectors, positive_shard.reshape(1, ROWS), positive_row.reshape(1, ROWS), negr,
        log_prob.reshape(1, ITEMS), item_table,
    )
    new_table, new_accum = update(negr, rows, coefs, gsum, ups, item_table, grad_accum)
    return (new_table, new_accum, loss.reshape(ROWS))


def solution(mesh):
    in_specs = (
        P(("item", "batch"), None),
        P("item", None),
        P("item", None),
        P("item"),
        P(("item", "batch"), None),
        P(("item", "batch")),
        P("item"),
    )
    out_specs = (P("item", None), P("item", None), P(("item", "batch")))
    return jax.shard_map(
        per_device, mesh=mesh, in_specs=in_specs, out_specs=out_specs, check_vma=False
    )
```

```python
import math

import jax
import jax.numpy as jnp
from jax import lax
from jax.experimental import pallas as pl
from jax.experimental.pallas import tpu as pltpu
from jax.sharding import PartitionSpec as P

LOGIT_SCALE = 2.5
STEP_RATE = 0.05
LOG2E = math.log2(math.e)
LN2 = math.log(2.0)
FLOOR = -1e30

BLOCKS = 128
ROWS = 128
WIDTH = 256
ITEMS = 2048
NEGS = 512
STEPS = 64
AHEAD = 1
SLOTS = 256


RING = (0, 1, 3, 2)


def order4(q):
    return jnp.where(q < 2, q, 5 - q)


def head_kernel(
    u_ref, shard_ref, row_ref, negr_ref, lp_ref, table_ref,
    gsum_ref, up_out, r_out, c_out, loss_ref,
    users, scores_own, scores_sib, negs, bias, tab, tabb, ids_all, slot_i, slot_r,
    slot_t, slot_lp, slot_pos, slot_u,
    stat_out, stat_in, norm_all, acc, gsend, grecv, upx, rx, cx,
    block_sem, send_sem, tab_sem, ids_sem, ids_send, stat_sem, stat_send, norm_sem, norm_send,
    pair_send, pair_recv,
):
    me = lax.axis_index("item")
    group = lax.axis_index("batch")
    other = 1 - group
    core = lax.rem(me, 2)
    sib = me + 1 - 2 * core
    x_pos = lax.rem(me // 2, 4)
    z_pos = lax.rem(me // 8, 4)
    y_pos = me // 32
    outer = jnp.where(core == 0, y_pos, x_pos)
    inner = jnp.where(core == 0, x_pos, y_pos)
    s_out = jnp.where(core == 0, 32, 2)
    s_in = 34 - s_out

    def place(do, di, dz):
        return (
            lax.rem(outer + do, 4) * s_out + lax.rem(inner + di, 4) * s_in
            + lax.rem(z_pos + dz, 4) * 8 + core
        )

    def sib_place(do, di, dz):
        return (
            lax.rem(inner + do, 4) * s_in + lax.rem(outer + di, 4) * s_out
            + lax.rem(z_pos + dz, 4) * 8 + 1 - core
        )

    barrier = pltpu.get_barrier_semaphore()
    pl.semaphore_signal(
        barrier, inc=1, device_id={"batch": other}, device_id_type=pl.DeviceIdType.MESH
    )

    def greet(dev):
        pl.semaphore_signal(
            barrier, inc=1, device_id={"item": dev}, device_id_type=pl.DeviceIdType.MESH
        )

    row_start = (me // 8) * 8

    @pl.loop(1, 8)
    def _(j):
        greet(row_start + lax.rem(me + j, 8))

    @pl.loop(1, 16)
    def _(j):
        greet(lax.rem(me + 8 * j, BLOCKS))

    table_copy = pltpu.make_async_copy(table_ref, tab, tab_sem)
    table_copy.start()
    users[me] = u_ref[...]
    ids_all[me] = shard_ref[...] * ITEMS + row_ref[...]
    pl.semaphore_wait(barrier, 23)

    def block_copy(b, dev):
        return pltpu.make_async_remote_copy(
            src_ref=users.at[b], dst_ref=users.at[b], send_sem=send_sem,
            recv_sem=block_sem.at[b], device_id={"item": dev},
            device_id_type=pl.DeviceIdType.MESH,
        )

    def arrived(b):
        block_copy(b, sib).wait_recv()

    def send(b, *devices):
        for dev in devices:
            block_copy(b, dev).start()

    out_up, out_down = place(1, 0, 0), place(3, 0, 0)
    in_up, in_down = place(0, 1, 0), place(0, 3, 0)
    z_up, z_down = place(0, 0, 1), place(0, 0, 3)

    def plane_block(ki, j):
        dz = RING[j]
        b = place(0, order4(ki), dz)
        if j == 0:

            @pl.when(ki > 0)
            def _():
                arrived(b)
        else:
            arrived(b)

        @pl.when(ki == 0)
        def _():
            if j == 0:
                send(b, z_down, z_up)
            if j == 2:
                far = place(0, 0, 1 + 2 * core)
                send(far, jnp.where(core == 0, z_down, z_up))
            send(b, in_down, in_up)

        send(b, out_down, out_up)

        @pl.when(ki == (1 if j % 2 == 0 else 2))
        def _():
            send(b, in_down if j % 2 == 0 else in_up)

        send(b, sib)

    def peer_copy(src, dst, send_to, recv, dev):
        return pltpu.make_async_remote_copy(
            src_ref=src, dst_ref=dst, send_sem=send_to, recv_sem=recv,
            device_id={"item": dev}, device_id_type=pl.DeviceIdType.MESH,
        )

    def wait_bytes(ref, sem):
        pltpu.make_async_copy(ref, ref, sem).wait()

    plane_block(jnp.int32(0), 0)

    @pl.loop(1, 8)
    def _(j):
        dev = row_start + lax.rem(me + j, 8)
        peer_copy(ids_all.at[me], ids_all.at[me], ids_send.at[0], ids_sem.at[0], dev).start()

    table_copy.wait()
    tabb[...] = tab[...].astype(jnp.bfloat16)
    lp2 = lp_ref[...] * LOG2E

    def gather(row_cols):
        lane = lax.broadcasted_iota(jnp.int32, row_cols.shape, 1)
        hots = [row_cols == lane + 128 * j for j in range(ITEMS // 128)]
        hot = jnp.concatenate([h.astype(jnp.float32).astype(jnp.bfloat16) for h in hots], axis=1)
        rows = jnp.dot(hot, tabb[...], preferred_element_type=jnp.float32)
        total = jnp.zeros(row_cols.shape, jnp.float32)
        for j, h in enumerate(hots):
            total = total + jnp.where(h, lp2[:, 128 * j : 128 * (j + 1)], 0.0)
        lp_rows = jnp.broadcast_to(jnp.sum(total, axis=1, keepdims=True), row_cols.shape)
        return rows, lp_rows

    wait_bytes(ids_all.at[pl.ds(0, 7)], ids_sem.at[0])
    ids_row = ids_all.at[pl.ds(row_start, 8)]

    @pl.loop(1, 16)
    def _(j):
        dev = lax.rem(me + 8 * j, BLOCKS)
        peer_copy(ids_row, ids_row, ids_send.at[1], ids_sem.at[1], dev).start()

    neg_cols = jnp.transpose(jnp.broadcast_to(negr_ref[...], (128, NEGS)))
    for q in range(NEGS // 128):
        part = slice(128 * q, 128 * (q + 1))
        rows, lp_rows = gather(neg_cols[part])
        negs[part, :] = rows.astype(jnp.bfloat16)
        bias[part, :] = lp_rows

    plane_block(jnp.int32(0), 1)
    plane_block(jnp.int32(0), 2)

    wait_bytes(ids_all.at[pl.ds(0, BLOCKS - 8)], ids_sem.at[1])
    ids = ids_all[:, 0, :]
    wide = (BLOCKS, ROWS)
    lane = lax.broadcasted_iota(jnp.int32, wide, 1)
    mine = (ids // ITEMS) == me
    row = lax.rem(ids, ITEMS)
    lo = jnp.broadcast_to(
        jnp.min(jnp.where(mine, lane, ROWS), axis=1, keepdims=True), wide
    )
    hi = jnp.broadcast_to(jnp.max(jnp.where(mine, lane, -1), axis=1, keepdims=True), wide)
    first = mine & (lane == lo)
    last = mine & (lane == hi) & (hi > lo)
    slot_i[0:BLOCKS, :] = jnp.where(lo < ROWS, lo, -1)
    slot_i[BLOCKS:, :] = jnp.where(hi > lo, hi, -1)
    for c, hit in enumerate((first, last)):
        slot_r[BLOCKS * c : BLOCKS * (c + 1), :] = jnp.broadcast_to(
            jnp.max(jnp.where(hit, row, -1), axis=1, keepdims=True), wide
        )
    for q in range(SLOTS // 128):
        part = slice(128 * q, 128 * (q + 1))
        rows, lp_rows = gather(slot_r[part, :])
        slot_t[part, :] = rows
        slot_lp[part, :] = lp_rows

    for q in range(3, 4 * AHEAD):
        plane_block(jnp.int32(q // 4), q % 4)

    sub = lax.broadcasted_iota(jnp.int32, (8, 128), 0)
    lane8 = lax.broadcasted_iota(jnp.int32, (8, 128), 1)

    def pick(values):
        out = jnp.broadcast_to(values[3], (8, values[3].shape[1]))
        s8 = lax.broadcasted_iota(jnp.int32, out.shape, 0)
        for c in (2, 1, 0):
            out = jnp.where(s8 == c, values[c], out)
        return out

    def tile_blocks(s):
        near = s - 8
        far = 2 * (s - 24)
        offsets = []
        for h in range(2):
            k = jnp.where(s < 8, 2 * s + h, jnp.where(s < 24, near, far + h))
            do = jnp.where(s < 8, 0, jnp.where(s < 24, 1 + 2 * h, 2))
            offsets.append((do, order4(k // 4), order4(lax.rem(k, 4))))
        return [place(*o) for o in offsets], [sib_place(*o) for o in offsets]

    def both_users(blocks):
        return jnp.concatenate([users[blocks[0]], users[blocks[1]]], axis=0)

    def score(blocks, scores):
        pair = both_users(blocks)
        a, b = blocks
        at = [a, BLOCKS + a, b, BLOCKS + b]
        index = [slot_i[pl.ds(r, 1), :] for r in at]
        left = jnp.where(sub == 0, index[0], jnp.where(sub == 1, index[1], -2)) == lane8
        right = jnp.where(sub == 2, index[2], jnp.where(sub == 3, index[3], -2)) == lane8
        mask = jnp.concatenate([jnp.where(left, 1.0, 0.0), jnp.where(right, 1.0, 0.0)], axis=1)
        hot = jnp.concatenate([mask, jnp.zeros_like(mask)], axis=0).astype(jnp.bfloat16)
        raw = lax.dot_general(
            negs[...], pair, (((1,), (1,)), ((), ())), preferred_element_type=jnp.float32
        )
        cols = bias[...]
        scaled = raw * (LOGIT_SCALE * LOG2E) - jnp.concatenate([cols, cols], axis=1)
        scores[a // 2] = scaled[:, :ROWS]
        scores[b // 2] = scaled[:, ROWS:]
        peak = jnp.max(scaled, axis=0, keepdims=True)
        gathered = jnp.dot(hot, pair, preferred_element_type=jnp.float32)[0:8]
        dots = jnp.sum(
            gathered * pick([slot_t[pl.ds(r, 1), :] for r in at]), axis=1, keepdims=True
        )
        pos = dots * (LOGIT_SCALE * LOG2E) - pick([slot_lp[pl.ds(r, 1), :] for r in at])
        for c, r in enumerate(at):
            slot_u[pl.ds(r, 1), :] = gathered[c : c + 1]
            slot_pos[pl.ds(r, 1), :] = pos[c : c + 1]
        pos_row = jnp.max(
            jnp.where(mask > 0.0, jnp.concatenate([pos, pos], axis=1), FLOOR),
            axis=0, keepdims=True,
        )
        return peak, pos_row

    def summed(blocks, scores, peak, pos_row):
        for h, b in enumerate(blocks):
            part = slice(ROWS * h, ROWS * (h + 1))
            total = jnp.sum(jnp.exp2(scores[b // 2] - peak[:, part]), axis=0, keepdims=True)
            lse = peak[:, part] + jnp.log(total) * LOG2E
            stat_out[b] = jnp.concatenate([lse, pos_row[:, part]], axis=0)

    def send_stats(b):
        peer_copy(stat_out.at[b], stat_in.at[me], stat_send, stat_sem, b).start()

    def tile(s):
        own, sibs = tile_blocks(s)
        for b in sibs:
            arrived(b)
        first_own = score(own, scores_own)
        first_sib = score(sibs, scores_sib)
        summed(own, scores_own, *first_own)
        summed(sibs, scores_sib, *first_sib)

        @pl.when(s > 0)
        def _():
            send_stats(own[0])

        send_stats(own[1])
        send_stats(sibs[0])
        send_stats(sibs[1])

    def far_block(ki, j):
        b = place(2, order4(ki), RING[j])
        arrived(b)
        send(b, sib)

    @pl.loop(0, 4)
    def _(m):
        for j in range(4):

            @pl.when(m < 4 - AHEAD)
            def _():
                plane_block(m + AHEAD, j)

            di, dz = order4(m), RING[j]
            b1, b3 = place(1, di, dz), place(3, di, dz)
            arrived(b1)
            if j % 2 == 0:
                send(b1, out_down)
            send(b1, sib)
            arrived(b3)
            if j % 2 == 1:
                send(b3, out_up)
            send(b3, sib)

            @pl.when(m > 0)
            def _():
                far_block(m - 1, j)

            k = 4 * m + j
            rest = 24 + (k - 6) // 2 if j % 2 == 0 else (k - 1) // 2

            @pl.loop(0, 2)
            def _(e):
                s = jnp.where(e == 0, k + 6, rest)

                @pl.when(k >= jnp.where(e == 0, 2, 6 if j % 2 == 0 else 0))
                def _():
                    tile(s)

    for j in range(4):
        far_block(3, j)

    @pl.loop(0, 5)
    def _(e):
        tile(jnp.where(e < 2, 22 + e, 27 + e))

    stat_in[me] = stat_out[me]

    def pair_copy(src, dst, k):
        return pltpu.make_async_remote_copy(
            src_ref=src, dst_ref=dst, send_sem=pair_send.at[k], recv_sem=pair_recv.at[k],
            device_id={"batch": other}, device_id_type=pl.DeviceIdType.MESH,
        )

    def to_lanes(cols):
        return jnp.concatenate(
            [jnp.transpose(cols[BLOCKS * c : BLOCKS * (c + 1)])[0:8, :] for c in range(2)], axis=1
        )

    wait_bytes(stat_in.at[pl.ds(0, BLOCKS - 1)], stat_sem)
    lses = stat_in[:, 0, :]
    pos_own = jnp.max(stat_in[:, 1, :], axis=0, keepdims=True)
    top = jnp.maximum(jnp.max(lses, axis=0, keepdims=True), pos_own)
    total = jnp.sum(jnp.exp2(lses - top), axis=0, keepdims=True) + jnp.exp2(pos_own - top)
    norm = top + jnp.log(total) * LOG2E
    norm_all[me] = norm

    @pl.loop(1, BLOCKS)
    def _(j):
        dev = lax.rem(me + j, BLOCKS)
        peer_copy(norm_all.at[me], norm_all.at[me], norm_send, norm_sem, dev).start()

    loss_ref[...] = (norm - pos_own) * LN2
    upx[group] = slot_u[...].astype(jnp.bfloat16)
    rx[group] = to_lanes(slot_r[...])
    up_copy = pair_copy(upx.at[group], upx.at[group], 0)
    r_copy = pair_copy(rx.at[group], rx.at[group], 1)
    up_copy.start()
    r_copy.start()
    wait_bytes(norm_all.at[pl.ds(0, BLOCKS - 1)], norm_sem)

    norms = norm_all[:, 0, :]
    lane = lax.broadcasted_iota(jnp.int32, wide, 1)
    coefs = []
    for c in range(2):
        part = slice(BLOCKS * c, BLOCKS * (c + 1))
        index = slot_i[part, :]
        found = jnp.sum(jnp.where(index == lane, norms, 0.0), axis=1, keepdims=True)
        coefficient = jnp.exp2(slot_pos[part, :] - found) - 1.0
        coefs.append(jnp.where(index >= 0, LOGIT_SCALE * coefficient, 0.0))
    cx[group] = to_lanes(jnp.concatenate(coefs, axis=0))
    c_copy = pair_copy(cx.at[group], cx.at[group], 2)
    c_copy.start()

    copies = [up_copy, r_copy, c_copy]
    half = NEGS // 2
    for h in range(2):
        part = slice(half * h, half * (h + 1))
        acc[...] = jnp.zeros_like(acc)

        @pl.loop(0, STEPS // 8)
        def _(g):
            probs, rows = [], []
            for u in range(8):
                c = 8 * g + u
                for scores, b in ((scores_own, 2 * c + core), (scores_sib, 2 * c + 1 - core)):
                    probs.append(
                        jnp.exp2(scores[c, part, :] - norm_all[b]).astype(jnp.bfloat16)
                    )
                    rows.append(users[b])
            acc[...] += jnp.dot(
                jnp.concatenate(probs, axis=1), jnp.concatenate(rows, axis=0),
                preferred_element_type=jnp.float32,
            )

        gsend[h] = acc[...].astype(gsend.dtype)
        g_copy = pair_copy(gsend.at[h], grecv.at[h], 3 + h)
        g_copy.start()
        copies.append(g_copy)

    for copy in copies:
        copy.wait()
    for h in range(2):
        part = slice(half * h, half * (h + 1))
        gsum_ref[part, :] = gsend[h].astype(jnp.float32) + grecv[h].astype(jnp.float32)
    for k in range(2):
        up_out[SLOTS * k : SLOTS * (k + 1), :] = upx[k]
        r_out[:, SLOTS * k : SLOTS * (k + 1)] = rx[k]
        c_out[:, SLOTS * k : SLOTS * (k + 1)] = cx[k]
    wait_bytes(users.at[pl.ds(0, BLOCKS - 1)], send_sem)
    wait_bytes(ids_all.at[pl.ds(0, 7)], ids_send.at[0])
    wait_bytes(ids_all.at[pl.ds(0, BLOCKS - 8)], ids_send.at[1])
    wait_bytes(stat_in.at[pl.ds(0, BLOCKS - 1)], stat_send)
    wait_bytes(norm_all.at[pl.ds(0, BLOCKS - 1)], norm_send)


def head(u, shards, rows, negr, lp, table):
    f32, bf16, i32 = jnp.float32, jnp.bfloat16, jnp.int32
    vmem = pl.BlockSpec(memory_space=pltpu.VMEM)
    dma = pltpu.SemaphoreType.DMA
    V = pltpu.VMEM
    return pl.pallas_call(
        head_kernel,
        out_shape=(
            jax.ShapeDtypeStruct((NEGS, WIDTH), f32),
            jax.ShapeDtypeStruct((2 * SLOTS, WIDTH), bf16),
            jax.ShapeDtypeStruct((8, 2 * SLOTS), i32),
            jax.ShapeDtypeStruct((8, 2 * SLOTS), f32),
            jax.ShapeDtypeStruct((1, ROWS), f32),
        ),
        in_specs=[vmem] * 5 + [pl.BlockSpec(memory_space=pl.ANY)],
        out_specs=(vmem,) * 5,
        scratch_shapes=[
            V((BLOCKS, ROWS, WIDTH), bf16),
            V((STEPS, NEGS, ROWS), f32),
            V((STEPS, NEGS, ROWS), f32),
            V((NEGS, WIDTH), bf16),
            V((NEGS, 128), f32),
            V((ITEMS, WIDTH), f32),
            V((ITEMS, WIDTH), bf16),
            V((BLOCKS, 1, ROWS), i32),
            V((SLOTS, 128), i32),
            V((SLOTS, 128), i32),
            V((SLOTS, WIDTH), f32),
            V((SLOTS, 128), f32),
            V((SLOTS, 128), f32),
            V((SLOTS, WIDTH), f32),
            V((BLOCKS, 2, ROWS), f32),
            V((BLOCKS, 2, ROWS), f32),
            V((BLOCKS, 1, ROWS), f32),
            V((NEGS // 2, WIDTH), f32),
            V((2, NEGS // 2, WIDTH), bf16),
            V((2, NEGS // 2, WIDTH), bf16),
            V((2, SLOTS, WIDTH), bf16),
            V((2, 8, SLOTS), i32),
            V((2, 8, SLOTS), f32),
            dma((BLOCKS,)),
            dma, dma, dma((2,)), dma((2,)), dma, dma, dma, dma,
            dma((5,)),
            dma((5,)),
        ],
        compiler_params=pltpu.CompilerParams(
            has_side_effects=True, vmem_limit_bytes=58 * 1024 * 1024, collective_id=0
        ),
        cost_estimate=pl.CostEstimate(
            flops=3 * 2 * 16384 * NEGS * WIDTH, bytes_accessed=4 << 20,
            transcendentals=2 * 16384 * NEGS,
        ),
        name="sampled_head",
    )(u, shards, rows, negr, lp, table)


TILE = 512


def update_kernel(
    negr_ref, r_ref, c_ref, gsum_ref, up_ref, table_ref, accum_ref,
    new_table_ref, new_accum_ref, g_hi, g_lo,
):
    @pl.when(pl.program_id(0) == 0)
    def _():
        g = LOGIT_SCALE * gsum_ref[...]
        top = g.astype(jnp.bfloat16)
        g_hi[...] = top
        g_lo[...] = (g - top.astype(jnp.float32)).astype(jnp.bfloat16)

    row = lax.broadcasted_iota(jnp.int32, (TILE, NEGS), 0) + TILE * pl.program_id(0)
    hot = jnp.where(row == negr_ref[...], 1.0, 0.0).astype(jnp.bfloat16)
    weight = jnp.where(row == r_ref[0:1, :], c_ref[0:1, :], 0.0)
    w_hi = weight.astype(jnp.bfloat16)
    w_lo = (weight - w_hi.astype(jnp.float32)).astype(jnp.bfloat16)

    def mm(a, b):
        return jnp.dot(a, b, preferred_element_type=jnp.float32)

    grad = (mm(hot, g_hi[...]) + mm(hot, g_lo[...])) + (
        mm(w_hi, up_ref[...]) + mm(w_lo, up_ref[...])
    )
    accum = accum_ref[...] + grad * grad
    new_accum_ref[...] = accum
    new_table_ref[...] = table_ref[...] - STEP_RATE * grad * lax.rsqrt(accum)


def update(negr, rows, coefs, gsum, ups, table, accum):
    whole = lambda shape: pl.BlockSpec(shape, lambda i: (0, 0))
    tile = pl.BlockSpec((TILE, WIDTH), lambda i: (i, 0))
    return pl.pallas_call(
        update_kernel,
        grid=(ITEMS // TILE,),
        out_shape=(jax.ShapeDtypeStruct((ITEMS, WIDTH), jnp.float32),) * 2,
        in_specs=[
            whole((1, NEGS)), whole((8, 2 * SLOTS)), whole((8, 2 * SLOTS)),
            whole((NEGS, WIDTH)), whole((2 * SLOTS, WIDTH)), tile, tile,
        ],
        out_specs=(tile, tile),
        scratch_shapes=[pltpu.VMEM((NEGS, WIDTH), jnp.bfloat16)] * 2,
        compiler_params=pltpu.CompilerParams(vmem_limit_bytes=60 * 1024 * 1024),
        name="table_update",
    )(negr, rows, coefs, gsum, ups, table, accum)


def per_device(
    user_vectors, item_table, grad_accum, log_prob, positive_shard, positive_row, negatives
):
    negr = negatives.reshape(1, NEGS)
    gsum, ups, rows, coefs, loss = head(
        user_vectors, positive_shard.reshape(1, ROWS), positive_row.reshape(1, ROWS), negr,
        log_prob.reshape(1, ITEMS), item_table,
    )
    new_table, new_accum = update(negr, rows, coefs, gsum, ups, item_table, grad_accum)
    return (new_table, new_accum, loss.reshape(ROWS))


def solution(mesh):
    in_specs = (
        P(("item", "batch"), None),
        P("item", None),
        P("item", None),
        P("item"),
        P(("item", "batch"), None),
        P(("item", "batch")),
        P("item"),
    )
    out_specs = (P("item", None), P("item", None), P(("item", "batch")))
    return jax.shard_map(
        per_device, mesh=mesh, in_specs=in_specs, out_specs=out_specs, check_vma=False
    )
```

```python
import math

import jax
import jax.numpy as jnp
from jax import lax
from jax.experimental import pallas as pl
from jax.experimental.pallas import tpu as pltpu
from jax.sharding import PartitionSpec as P

LOGIT_SCALE = 2.5
STEP_RATE = 0.05
LOG2E = math.log2(math.e)
LN2 = math.log(2.0)
FLOOR = -1e30

BLOCKS = 128
ROWS = 128
WIDTH = 256
ITEMS = 2048
NEGS = 512
STEPS = 64
AHEAD = 1
SLOTS = 256


RING = (0, 1, 3, 2)


def order4(q):
    return jnp.where(q < 2, q, 5 - q)


def head_kernel(
    u_ref, shard_ref, row_ref, negr_ref, lp_ref, table_ref,
    gsum_ref, up_out, r_out, c_out, loss_ref,
    users, scores_own, scores_sib, negs, bias, tab, tabb, ids_all, slot_i, slot_r,
    slot_t, slot_lp, slot_pos, slot_u,
    stat_out, stat_in, norm_all, acc, gsend, grecv, upx, rx, cx,
    block_sem, send_sem, tab_sem, ids_sem, ids_send, stat_sem, stat_send, norm_sem, norm_send,
    pair_send, pair_recv,
):
    me = lax.axis_index("item")
    group = lax.axis_index("batch")
    other = 1 - group
    core = lax.rem(me, 2)
    sib = me + 1 - 2 * core
    x_pos = lax.rem(me // 2, 4)
    z_pos = lax.rem(me // 8, 4)
    y_pos = me // 32
    outer = jnp.where(core == 0, y_pos, x_pos)
    inner = jnp.where(core == 0, x_pos, y_pos)
    s_out = jnp.where(core == 0, 32, 2)
    s_in = 34 - s_out

    def place(do, di, dz):
        return (
            lax.rem(outer + do, 4) * s_out + lax.rem(inner + di, 4) * s_in
            + lax.rem(z_pos + dz, 4) * 8 + core
        )

    def sib_place(do, di, dz):
        return (
            lax.rem(inner + do, 4) * s_in + lax.rem(outer + di, 4) * s_out
            + lax.rem(z_pos + dz, 4) * 8 + 1 - core
        )

    barrier = pltpu.get_barrier_semaphore()
    pl.semaphore_signal(
        barrier, inc=1, device_id={"batch": other}, device_id_type=pl.DeviceIdType.MESH
    )

    def greet(dev):
        pl.semaphore_signal(
            barrier, inc=1, device_id={"item": dev}, device_id_type=pl.DeviceIdType.MESH
        )

    row_start = (me // 8) * 8

    @pl.loop(1, 8)
    def _(j):
        greet(row_start + lax.rem(me + j, 8))

    @pl.loop(1, 16)
    def _(j):
        greet(lax.rem(me + 8 * j, BLOCKS))

    table_copy = pltpu.make_async_copy(table_ref, tab, tab_sem)
    table_copy.start()
    users[me] = u_ref[...]
    ids_all[me] = shard_ref[...] * ITEMS + row_ref[...]
    pl.semaphore_wait(barrier, 23)

    def block_copy(b, dev):
        return pltpu.make_async_remote_copy(
            src_ref=users.at[b], dst_ref=users.at[b], send_sem=send_sem,
            recv_sem=block_sem.at[b], device_id={"item": dev},
            device_id_type=pl.DeviceIdType.MESH,
        )

    def arrived(b):
        block_copy(b, sib).wait_recv()

    def send(b, *devices):
        for dev in devices:
            block_copy(b, dev).start()

    out_up, out_down = place(1, 0, 0), place(3, 0, 0)
    in_up, in_down = place(0, 1, 0), place(0, 3, 0)
    z_up, z_down = place(0, 0, 1), place(0, 0, 3)

    def plane_block(ki, j):
        dz = RING[j]
        b = place(0, order4(ki), dz)
        if j == 0:

            @pl.when(ki > 0)
            def _():
                arrived(b)
        else:
            arrived(b)

        @pl.when(ki == 0)
        def _():
            if j == 0:
                send(b, z_down, z_up)
            if j == 2:
                far = place(0, 0, 1 + 2 * core)
                send(far, jnp.where(core == 0, z_down, z_up))
            send(b, in_down, in_up)

        send(b, out_down, out_up)

        @pl.when(ki == (1 if j % 2 == 0 else 2))
        def _():
            send(b, in_down if j % 2 == 0 else in_up)

        send(b, sib)

    def peer_copy(src, dst, send_to, recv, dev):
        return pltpu.make_async_remote_copy(
            src_ref=src, dst_ref=dst, send_sem=send_to, recv_sem=recv,
            device_id={"item": dev}, device_id_type=pl.DeviceIdType.MESH,
        )

    def wait_bytes(ref, sem):
        pltpu.make_async_copy(ref, ref, sem).wait()

    plane_block(jnp.int32(0), 0)

    @pl.loop(1, 8)
    def _(j):
        dev = row_start + lax.rem(me + j, 8)
        peer_copy(ids_all.at[me], ids_all.at[me], ids_send.at[0], ids_sem.at[0], dev).start()

    table_copy.wait()
    tabb[...] = tab[...].astype(jnp.bfloat16)
    lp2 = lp_ref[...] * LOG2E

    def gather(row_cols):
        lane = lax.broadcasted_iota(jnp.int32, row_cols.shape, 1)
        hots = [row_cols == lane + 128 * j for j in range(ITEMS // 128)]
        hot = jnp.concatenate([h.astype(jnp.float32).astype(jnp.bfloat16) for h in hots], axis=1)
        rows = jnp.dot(hot, tabb[...], preferred_element_type=jnp.float32)
        total = jnp.zeros(row_cols.shape, jnp.float32)
        for j, h in enumerate(hots):
            total = total + jnp.where(h, lp2[:, 128 * j : 128 * (j + 1)], 0.0)
        lp_rows = jnp.broadcast_to(jnp.sum(total, axis=1, keepdims=True), row_cols.shape)
        return rows, lp_rows

    wait_bytes(ids_all.at[pl.ds(0, 7)], ids_sem.at[0])
    ids_row = ids_all.at[pl.ds(row_start, 8)]

    @pl.loop(1, 16)
    def _(j):
        dev = lax.rem(me + 8 * j, BLOCKS)
        peer_copy(ids_row, ids_row, ids_send.at[1], ids_sem.at[1], dev).start()

    neg_cols = jnp.transpose(jnp.broadcast_to(negr_ref[...], (128, NEGS)))
    for q in range(NEGS // 128):
        part = slice(128 * q, 128 * (q + 1))
        rows, lp_rows = gather(neg_cols[part])
        negs[part, :] = rows.astype(jnp.bfloat16)
        bias[part, :] = lp_rows

    plane_block(jnp.int32(0), 1)
    plane_block(jnp.int32(0), 2)

    wait_bytes(ids_all.at[pl.ds(0, BLOCKS - 8)], ids_sem.at[1])
    ids = ids_all[:, 0, :]
    wide = (BLOCKS, ROWS)
    lane = lax.broadcasted_iota(jnp.int32, wide, 1)
    mine = (ids // ITEMS) == me
    row = lax.rem(ids, ITEMS)
    lo = jnp.broadcast_to(
        jnp.min(jnp.where(mine, lane, ROWS), axis=1, keepdims=True), wide
    )
    hi = jnp.broadcast_to(jnp.max(jnp.where(mine, lane, -1), axis=1, keepdims=True), wide)
    first = mine & (lane == lo)
    last = mine & (lane == hi) & (hi > lo)
    slot_i[0:BLOCKS, :] = jnp.where(lo < ROWS, lo, -1)
    slot_i[BLOCKS:, :] = jnp.where(hi > lo, hi, -1)
    for c, hit in enumerate((first, last)):
        slot_r[BLOCKS * c : BLOCKS * (c + 1), :] = jnp.broadcast_to(
            jnp.max(jnp.where(hit, row, -1), axis=1, keepdims=True), wide
        )
    for q in range(SLOTS // 128):
        part = slice(128 * q, 128 * (q + 1))
        rows, lp_rows = gather(slot_r[part, :])
        slot_t[part, :] = rows
        slot_lp[part, :] = lp_rows

    for q in range(3, 4 * AHEAD):
        plane_block(jnp.int32(q // 4), q % 4)

    sub = lax.broadcasted_iota(jnp.int32, (8, 128), 0)
    lane8 = lax.broadcasted_iota(jnp.int32, (8, 128), 1)

    def pick(values):
        out = jnp.broadcast_to(values[3], (8, values[3].shape[1]))
        s8 = lax.broadcasted_iota(jnp.int32, out.shape, 0)
        for c in (2, 1, 0):
            out = jnp.where(s8 == c, values[c], out)
        return out

    def tile_blocks(s):
        near = s - 8
        far = 2 * (s - 24)
        offsets = []
        for h in range(2):
            k = jnp.where(s < 8, 2 * s + h, jnp.where(s < 24, near, far + h))
            do = jnp.where(s < 8, 0, jnp.where(s < 24, 1 + 2 * h, 2))
            offsets.append((do, order4(k // 4), order4(lax.rem(k, 4))))
        return [place(*o) for o in offsets], [sib_place(*o) for o in offsets]

    def both_users(blocks):
        return jnp.concatenate([users[blocks[0]], users[blocks[1]]], axis=0)

    def score(blocks, scores):
        pair = both_users(blocks)
        a, b = blocks
        at = [a, BLOCKS + a, b, BLOCKS + b]
        index = [slot_i[pl.ds(r, 1), :] for r in at]
        left = jnp.where(sub == 0, index[0], jnp.where(sub == 1, index[1], -2)) == lane8
        right = jnp.where(sub == 2, index[2], jnp.where(sub == 3, index[3], -2)) == lane8
        mask = jnp.concatenate([jnp.where(left, 1.0, 0.0), jnp.where(right, 1.0, 0.0)], axis=1)
        hot = jnp.concatenate([mask, jnp.zeros_like(mask)], axis=0).astype(jnp.bfloat16)
        raw = lax.dot_general(
            negs[...], pair, (((1,), (1,)), ((), ())), preferred_element_type=jnp.float32
        )
        cols = bias[...]
        scaled = raw * (LOGIT_SCALE * LOG2E) - jnp.concatenate([cols, cols], axis=1)
        scores[a // 2] = scaled[:, :ROWS]
        scores[b // 2] = scaled[:, ROWS:]
        peak = jnp.max(scaled, axis=0, keepdims=True)
        gathered = jnp.dot(hot, pair, preferred_element_type=jnp.float32)[0:8]
        dots = jnp.sum(
            gathered * pick([slot_t[pl.ds(r, 1), :] for r in at]), axis=1, keepdims=True
        )
        pos = dots * (LOGIT_SCALE * LOG2E) - pick([slot_lp[pl.ds(r, 1), :] for r in at])
        for c, r in enumerate(at):
            slot_u[pl.ds(r, 1), :] = gathered[c : c + 1]
            slot_pos[pl.ds(r, 1), :] = pos[c : c + 1]
        pos_row = jnp.max(
            jnp.where(mask > 0.0, jnp.concatenate([pos, pos], axis=1), FLOOR),
            axis=0, keepdims=True,
        )
        return peak, pos_row

    def summed(blocks, scores, peak, pos_row):
        for h, b in enumerate(blocks):
            part = slice(ROWS * h, ROWS * (h + 1))
            total = jnp.sum(jnp.exp2(scores[b // 2] - peak[:, part]), axis=0, keepdims=True)
            lse = peak[:, part] + jnp.log(total) * LOG2E
            stat_out[b] = jnp.concatenate([lse, pos_row[:, part]], axis=0)

    def send_stats(b):
        peer_copy(stat_out.at[b], stat_in.at[me], stat_send, stat_sem, b).start()

    def tiles(*several):
        found = [tile_blocks(s) for s in several]
        for _, sibs in found:
            for b in sibs:
                arrived(b)
        halves = []
        for own, sibs in found:
            halves.append((own, scores_own, score(own, scores_own)))
            halves.append((sibs, scores_sib, score(sibs, scores_sib)))
        for blocks, scores, made in halves:
            summed(blocks, scores, *made)
        for s, (own, sibs) in zip(several, found):

            @pl.when(s > 0)
            def _():
                send_stats(own[0])

            send_stats(own[1])
            send_stats(sibs[0])
            send_stats(sibs[1])

    def far_block(ki, j):
        b = place(2, order4(ki), RING[j])
        arrived(b)
        send(b, sib)

    @pl.loop(0, 4)
    def _(m):
        for j in range(4):

            @pl.when(m < 4 - AHEAD)
            def _():
                plane_block(m + AHEAD, j)

            di, dz = order4(m), RING[j]
            b1, b3 = place(1, di, dz), place(3, di, dz)
            arrived(b1)
            if j % 2 == 0:
                send(b1, out_down)
            send(b1, sib)
            arrived(b3)
            if j % 2 == 1:
                send(b3, out_up)
            send(b3, sib)

            @pl.when(m > 0)
            def _():
                far_block(m - 1, j)

            k = 4 * m + j
            rest = 24 + (k - 6) // 2 if j % 2 == 0 else (k - 1) // 2

            least = (6, 3, 6, 3)[j]

            @pl.when(k >= least)
            def _():
                tiles(k + 6, rest)

            if j < 3:

                @pl.when((k > 0) & (k < least))
                def _():
                    tiles(rest if j == 1 else k + 6)

    for j in range(4):
        far_block(3, j)

    @pl.loop(0, 2)
    def _(e):
        tiles(22 + 7 * e, 23 + 7 * e)

    tiles(jnp.int32(31))

    stat_in[me] = stat_out[me]

    def pair_copy(src, dst, k):
        return pltpu.make_async_remote_copy(
            src_ref=src, dst_ref=dst, send_sem=pair_send.at[k], recv_sem=pair_recv.at[k],
            device_id={"batch": other}, device_id_type=pl.DeviceIdType.MESH,
        )

    def to_lanes(cols):
        return jnp.concatenate(
            [jnp.transpose(cols[BLOCKS * c : BLOCKS * (c + 1)])[0:8, :] for c in range(2)], axis=1
        )

    wait_bytes(stat_in.at[pl.ds(0, BLOCKS - 1)], stat_sem)
    lses = stat_in[:, 0, :]
    pos_own = jnp.max(stat_in[:, 1, :], axis=0, keepdims=True)
    top = jnp.maximum(jnp.max(lses, axis=0, keepdims=True), pos_own)
    total = jnp.sum(jnp.exp2(lses - top), axis=0, keepdims=True) + jnp.exp2(pos_own - top)
    norm = top + jnp.log(total) * LOG2E
    norm_all[me] = norm

    @pl.loop(1, BLOCKS)
    def _(j):
        dev = lax.rem(me + j, BLOCKS)
        peer_copy(norm_all.at[me], norm_all.at[me], norm_send, norm_sem, dev).start()

    loss_ref[...] = (norm - pos_own) * LN2
    upx[group] = slot_u[...].astype(jnp.bfloat16)
    rx[group] = to_lanes(slot_r[...])
    up_copy = pair_copy(upx.at[group], upx.at[group], 0)
    r_copy = pair_copy(rx.at[group], rx.at[group], 1)
    up_copy.start()
    r_copy.start()
    wait_bytes(norm_all.at[pl.ds(0, BLOCKS - 1)], norm_sem)

    norms = norm_all[:, 0, :]
    lane = lax.broadcasted_iota(jnp.int32, wide, 1)
    coefs = []
    for c in range(2):
        part = slice(BLOCKS * c, BLOCKS * (c + 1))
        index = slot_i[part, :]
        found = jnp.sum(jnp.where(index == lane, norms, 0.0), axis=1, keepdims=True)
        coefficient = jnp.exp2(slot_pos[part, :] - found) - 1.0
        coefs.append(jnp.where(index >= 0, LOGIT_SCALE * coefficient, 0.0))
    cx[group] = to_lanes(jnp.concatenate(coefs, axis=0))
    c_copy = pair_copy(cx.at[group], cx.at[group], 2)
    c_copy.start()

    copies = [up_copy, r_copy, c_copy]
    half = NEGS // 2
    for h in range(2):
        part = slice(half * h, half * (h + 1))
        acc[...] = jnp.zeros_like(acc)

        @pl.loop(0, STEPS // 8)
        def _(g):
            probs, rows = [], []
            for u in range(8):
                c = 8 * g + u
                for scores, b in ((scores_own, 2 * c + core), (scores_sib, 2 * c + 1 - core)):
                    probs.append(
                        jnp.exp2(scores[c, part, :] - norm_all[b]).astype(jnp.bfloat16)
                    )
                    rows.append(users[b])
            acc[...] += jnp.dot(
                jnp.concatenate(probs, axis=1), jnp.concatenate(rows, axis=0),
                preferred_element_type=jnp.float32,
            )

        gsend[h] = acc[...].astype(gsend.dtype)
        g_copy = pair_copy(gsend.at[h], grecv.at[h], 3 + h)
        g_copy.start()
        copies.append(g_copy)

    for copy in copies:
        copy.wait()
    for h in range(2):
        part = slice(half * h, half * (h + 1))
        gsum_ref[part, :] = gsend[h].astype(jnp.float32) + grecv[h].astype(jnp.float32)
    for k in range(2):
        up_out[SLOTS * k : SLOTS * (k + 1), :] = upx[k]
        r_out[:, SLOTS * k : SLOTS * (k + 1)] = rx[k]
        c_out[:, SLOTS * k : SLOTS * (k + 1)] = cx[k]
    wait_bytes(users.at[pl.ds(0, BLOCKS - 1)], send_sem)
    wait_bytes(ids_all.at[pl.ds(0, 7)], ids_send.at[0])
    wait_bytes(ids_all.at[pl.ds(0, BLOCKS - 8)], ids_send.at[1])
    wait_bytes(stat_in.at[pl.ds(0, BLOCKS - 1)], stat_send)
    wait_bytes(norm_all.at[pl.ds(0, BLOCKS - 1)], norm_send)


def head(u, shards, rows, negr, lp, table):
    f32, bf16, i32 = jnp.float32, jnp.bfloat16, jnp.int32
    vmem = pl.BlockSpec(memory_space=pltpu.VMEM)
    dma = pltpu.SemaphoreType.DMA
    V = pltpu.VMEM
    return pl.pallas_call(
        head_kernel,
        out_shape=(
            jax.ShapeDtypeStruct((NEGS, WIDTH), f32),
            jax.ShapeDtypeStruct((2 * SLOTS, WIDTH), bf16),
            jax.ShapeDtypeStruct((8, 2 * SLOTS), i32),
            jax.ShapeDtypeStruct((8, 2 * SLOTS), f32),
            jax.ShapeDtypeStruct((1, ROWS), f32),
        ),
        in_specs=[vmem] * 5 + [pl.BlockSpec(memory_space=pl.ANY)],
        out_specs=(vmem,) * 5,
        scratch_shapes=[
            V((BLOCKS, ROWS, WIDTH), bf16),
            V((STEPS, NEGS, ROWS), f32),
            V((STEPS, NEGS, ROWS), f32),
            V((NEGS, WIDTH), bf16),
            V((NEGS, 128), f32),
            V((ITEMS, WIDTH), f32),
            V((ITEMS, WIDTH), bf16),
            V((BLOCKS, 1, ROWS), i32),
            V((SLOTS, 128), i32),
            V((SLOTS, 128), i32),
            V((SLOTS, WIDTH), f32),
            V((SLOTS, 128), f32),
            V((SLOTS, 128), f32),
            V((SLOTS, WIDTH), f32),
            V((BLOCKS, 2, ROWS), f32),
            V((BLOCKS, 2, ROWS), f32),
            V((BLOCKS, 1, ROWS), f32),
            V((NEGS // 2, WIDTH), f32),
            V((2, NEGS // 2, WIDTH), bf16),
            V((2, NEGS // 2, WIDTH), bf16),
            V((2, SLOTS, WIDTH), bf16),
            V((2, 8, SLOTS), i32),
            V((2, 8, SLOTS), f32),
            dma((BLOCKS,)),
            dma, dma, dma((2,)), dma((2,)), dma, dma, dma, dma,
            dma((5,)),
            dma((5,)),
        ],
        compiler_params=pltpu.CompilerParams(
            has_side_effects=True, vmem_limit_bytes=58 * 1024 * 1024, collective_id=0
        ),
        cost_estimate=pl.CostEstimate(
            flops=3 * 2 * 16384 * NEGS * WIDTH, bytes_accessed=4 << 20,
            transcendentals=2 * 16384 * NEGS,
        ),
        name="sampled_head",
    )(u, shards, rows, negr, lp, table)


TILE = 512


def update_kernel(
    negr_ref, r_ref, c_ref, gsum_ref, up_ref, table_ref, accum_ref,
    new_table_ref, new_accum_ref, g_hi, g_lo,
):
    @pl.when(pl.program_id(0) == 0)
    def _():
        g = LOGIT_SCALE * gsum_ref[...]
        top = g.astype(jnp.bfloat16)
        g_hi[...] = top
        g_lo[...] = (g - top.astype(jnp.float32)).astype(jnp.bfloat16)

    row = lax.broadcasted_iota(jnp.int32, (TILE, NEGS), 0) + TILE * pl.program_id(0)
    hot = jnp.where(row == negr_ref[...], 1.0, 0.0).astype(jnp.bfloat16)
    weight = jnp.where(row == r_ref[0:1, :], c_ref[0:1, :], 0.0)
    w_hi = weight.astype(jnp.bfloat16)
    w_lo = (weight - w_hi.astype(jnp.float32)).astype(jnp.bfloat16)

    def mm(a, b):
        return jnp.dot(a, b, preferred_element_type=jnp.float32)

    grad = (mm(hot, g_hi[...]) + mm(hot, g_lo[...])) + (
        mm(w_hi, up_ref[...]) + mm(w_lo, up_ref[...])
    )
    accum = accum_ref[...] + grad * grad
    new_accum_ref[...] = accum
    new_table_ref[...] = table_ref[...] - STEP_RATE * grad * lax.rsqrt(accum)


def update(negr, rows, coefs, gsum, ups, table, accum):
    whole = lambda shape: pl.BlockSpec(shape, lambda i: (0, 0))
    tile = pl.BlockSpec((TILE, WIDTH), lambda i: (i, 0))
    return pl.pallas_call(
        update_kernel,
        grid=(ITEMS // TILE,),
        out_shape=(jax.ShapeDtypeStruct((ITEMS, WIDTH), jnp.float32),) * 2,
        in_specs=[
            whole((1, NEGS)), whole((8, 2 * SLOTS)), whole((8, 2 * SLOTS)),
            whole((NEGS, WIDTH)), whole((2 * SLOTS, WIDTH)), tile, tile,
        ],
        out_specs=(tile, tile),
        scratch_shapes=[pltpu.VMEM((NEGS, WIDTH), jnp.bfloat16)] * 2,
        compiler_params=pltpu.CompilerParams(vmem_limit_bytes=60 * 1024 * 1024),
        name="table_update",
    )(negr, rows, coefs, gsum, ups, table, accum)


def per_device(
    user_vectors, item_table, grad_accum, log_prob, positive_shard, positive_row, negatives
):
    negr = negatives.reshape(1, NEGS)
    gsum, ups, rows, coefs, loss = head(
        user_vectors, positive_shard.reshape(1, ROWS), positive_row.reshape(1, ROWS), negr,
        log_prob.reshape(1, ITEMS), item_table,
    )
    new_table, new_accum = update(negr, rows, coefs, gsum, ups, item_table, grad_accum)
    return (new_table, new_accum, loss.reshape(ROWS))


def solution(mesh):
    in_specs = (
        P(("item", "batch"), None),
        P("item", None),
        P("item", None),
        P("item"),
        P(("item", "batch"), None),
        P(("item", "batch")),
        P("item"),
    )
    out_specs = (P("item", None), P("item", None), P(("item", "batch")))
    return jax.shard_map(
        per_device, mesh=mesh, in_specs=in_specs, out_specs=out_specs, check_vma=False
    )
```
